1024 devices in a mesh: row: 64 (over z, core), col: 16 (over x, y).
Axes of the slice: x: 4, y: 4, z: 32, core: 2. Of those that a mesh axis runs over, the one named last changes fastest.
Arguments:
- grad_out: bfloat16 [131072, 256], P(('col', 'row')), may hold values from -384 to 384
- features: bfloat16 [131072, 256], P(('row', 'col')), may hold values from -24 to 24
- weight: bfloat16 [256, 256], replicated, may hold values from -0.375 to 0.375
- tile_values: bfloat16 [64, 16, 80, 128, 128], P('row', 'col'), may hold values from 0 to 0.00048828125
- tile_rows: int32 [64, 16, 80], P('row', 'col'), may hold values from 0 to 15
- tile_cols: int32 [64, 16, 80], P('row', 'col'), may hold values from 0 to 63
- tile_count: int32 [64, 16], P('row', 'col'), may hold values from 20 to 80, as said below
Outputs:
- input_grad: bfloat16 [131072, 256], P(('row', 'col'))
- weight_grad: float32 [256, 256], replicated
The draws below stay inside these ranges and needn't reach their ends.
Inputs may be any that keep to these rules, and one draw needn't show every extreme that they name: Live slots of a block are its first tile_count entries; every draw has blocks with all 80 slots live.
All inputs are finite; a program needn't handle non-finite values.
Results may differ from the reference program's by a relative error of at most 0.0049.
Values may be sent and summed in bfloat16 or wider, within the bound.
No kernel may reach another device: no remote copies, remote signals or barrier semaphores. Data moves between devices by JAX's collectives and lax.ppermute only.
A program may use at most 32 MiB of HBM per device.

```python
import jax
import jax.numpy as jnp
from jax import lax

D = 256
TILE = 128
TILES_DEV = 80
NODES = 131072
ROW_TILES = 16
COL_TILES = 64
N_ROW = 64
N_COL = 16


def draw_tile_count(key, part):
    key = jax.random.fold_in(key, 7)
    first, second = jax.random.split(key)
    blocks = N_ROW * N_COL
    base = jax.random.randint(first, (N_ROW, N_COL), TILES_DEV // 4, TILES_DEV // 2 + 1)
    order = jax.random.permutation(second, blocks).reshape(N_ROW, N_COL)
    heavy = order < max(1, blocks // 16)
    return jnp.where(heavy, TILES_DEV, base).astype(jnp.int32)


def with_ends(entries, rng, least, high):
    dims = entries.shape
    place = [jax.random.randint(jax.random.fold_in(rng, axis), (), 0, dims[axis]) for axis in range(len(dims))]
    entries = entries.at[tuple(place)].set(least)
    longest = dims.index(max(dims))
    place[longest] = (place[longest] + 1) % dims[longest]
    return entries.at[tuple(place)].set(high)


def raised(drawn, key, source, target, shards_of, factor):
    owner, partner = [(jnp.arange(drawn.shape[position]) // (drawn.shape[position] // shards_of)).reshape([-1 if axis == position else 1 for axis in range(drawn.ndim)]) for position in (source, target)]
    chosen = jax.random.permutation(key, shards_of)[partner]
    strong = (owner == chosen) | (owner == (partner + shards_of // 2) % shards_of)
    return jnp.where(strong, factor * drawn, drawn)


def block_levels(stream_key, shape, shards, least, largest):
    level, own = 1.0, jax.random.fold_in(stream_key, 6)
    for axis_at, blocks in shards:
        draws = jnp.exp(jax.random.uniform(jax.random.fold_in(own, axis_at), (blocks,), jnp.float32, least / len(shards), largest / len(shards)))
        level = level * jnp.repeat(draws, shape[axis_at] // blocks).reshape([-1 if axis == axis_at else 1 for axis in range(len(shape))])
    return level


def bell_draw(stream_key, extent, width, reach, cuts=(), kind=jnp.bfloat16):
    entries = jax.random.normal(stream_key, extent, jnp.float32) * width
    if len(cuts) > 0:
        entries = block_levels(stream_key, extent, cuts, -0.22, 0.18) * entries
    return jnp.clip(entries, min=-reach, max=reach).astype(kind)


def heavy_noise(stream_key, dims, deviation, limit, cuts, heavy, kind=jnp.bfloat16):
    array = deviation * jax.random.normal(stream_key, dims, jnp.float32)
    if cuts:
        array = array * block_levels(stream_key, dims, cuts, -0.22, 0.18)
    return jnp.clip(raised(array, jax.random.fold_in(stream_key, 3), *heavy), -limit, limit).astype(kind)


def setup_inputs(seed: int = 0) -> dict:
    splits = jax.random.split(jax.random.key(seed), 8)
    return {
        "grad_out": bell_draw(splits[0], (NODES, D), ((2 * N_COL * TILES_DEV * TILE // (5 * ROW_TILES)) ** 0.5), 384.0, ((0, 1024),)),
        "features": heavy_noise(splits[1], (NODES, D), 1.0, 24.0, ((0, 1024),), (0, 1, 256, 6.0)),
        "weight": bell_draw(splits[2], (D, D), D ** -0.5, 0.375),
        "tile_values": jnp.clip(0.00048828125 * jax.random.uniform(splits[3], (N_ROW, N_COL, TILES_DEV, TILE, TILE), jnp.float32) ** block_levels(splits[3], (N_ROW, N_COL, TILES_DEV, TILE, TILE), ((0, 64), (1, 16)), -0.2, 0.2), 0.0, 0.00048828125).astype(jnp.bfloat16),
        "tile_rows": with_ends(jax.random.randint(splits[4], (N_ROW, N_COL, TILES_DEV), 0, ROW_TILES), jax.random.fold_in(splits[4], 1), 0, ROW_TILES - 1).astype(jnp.int32),
        "tile_cols": with_ends(jax.random.randint(splits[5], (N_ROW, N_COL, TILES_DEV), 0, COL_TILES), jax.random.fold_in(splits[5], 1), 0, COL_TILES - 1).astype(jnp.int32),
        "tile_count": draw_tile_count(jax.random.fold_in(splits[7], 71), 0),
    }


def block_term(values, rows_of, cols_of, count, col_blocks):
    live = jnp.arange(values.shape[0], dtype=jnp.int32) < count
    picked = col_blocks[cols_of].astype(jnp.float32)
    prods = jnp.einsum("gij,gjw->giw", values.astype(jnp.float32), picked, precision=lax.Precision.HIGHEST)
    placing = ((rows_of[:, None] == jnp.arange(ROW_TILES, dtype=jnp.int32)[None, :]) & live[:, None]).astype(jnp.float32)
    return jnp.einsum("gr,giw->riw", placing, prods, precision=lax.Precision.HIGHEST)


def reference(grad_out, features, weight, tile_values, tile_rows, tile_cols, tile_count):
    blocks = grad_out.reshape(N_COL, COL_TILES, TILE, D)

    def row_block(index):
        def over_cols(total, other):
            term = block_term(tile_values[index, other], tile_rows[index, other], tile_cols[index, other], tile_count[index, other], blocks[other])
            return total + term, None

        start = jnp.zeros((ROW_TILES, TILE, D), jnp.float32)
        total, unused = lax.scan(over_cols, start, jnp.arange(N_COL, dtype=jnp.int32))
        return total

    carried = lax.map(row_block, jnp.arange(N_ROW, dtype=jnp.int32)).reshape(NODES, D)
    carried_b = carried.astype(jnp.bfloat16)
    input_grad = jnp.dot(carried_b, weight.T, preferred_element_type=jnp.float32).astype(jnp.bfloat16)
    weight_grad = jnp.dot(features.T, carried_b, preferred_element_type=jnp.float32) * (NODES ** -0.5)
    return input_grad, weight_grad
```

```python
import functools

import jax
import jax.numpy as jnp
from jax import lax
from jax.experimental import pallas as pl
from jax.experimental.pallas import tpu as pltpu
from jax.sharding import Mesh
from jax.sharding import PartitionSpec as P

ROW = ("zh", "zm", "zl", "core")
COL = ("x", "y")


def tiles_kernel(count_ref, rows_ref, cols_ref, values_ref, gathered_ref, features_ref, out_ref, total):
    row_tiles, tile, width = total.shape
    share = features_ref.shape[1] // row_tiles
    total[...] = jnp.zeros_like(total)

    def add(slot):
        row = rows_ref[slot]
        total[row] += jnp.dot(
            values_ref[slot], gathered_ref[cols_ref[slot]], preferred_element_type=jnp.float32
        )

    count = count_ref[0]
    fours = lax.shift_right_logical(count, 2)

    def four(index, carry):
        for offset in range(4):
            add(4 * index + offset)
        return carry

    def one(slot, carry):
        add(slot)
        return carry

    lax.fori_loop(0, fours, four, 0)
    lax.fori_loop(4 * fours, count, one, 0)

    step = 4
    grad = jnp.zeros((features_ref.shape[1], width), jnp.float32)
    for first in range(0, row_tiles, step):
        part = total[first : first + step].astype(jnp.bfloat16)
        out_ref[first : first + step, :tile] = part
        grad += lax.dot_general(
            features_ref[first * tile : (first + step) * tile],
            part.reshape(step * tile, width),
            (((0,), (0,)), ((), ())),
            preferred_element_type=jnp.float32,
        )
    out_ref[:, tile:] = grad.astype(jnp.bfloat16).reshape(row_tiles, share, width)


def finish_kernel(scale, parts_ref, weight_ref, input_ref, share_ref):
    tile = input_ref.shape[0]
    summed = parts_ref[0].astype(jnp.float32)
    for other in range(1, parts_ref.shape[0]):
        summed += parts_ref[other].astype(jnp.float32)
    share_ref[...] = summed[tile:] * scale
    input_ref[...] = lax.dot_general(
        summed[:tile].astype(jnp.bfloat16),
        weight_ref[...],
        (((1,), (1,)), ((), ())),
        preferred_element_type=jnp.float32,
    ).astype(jnp.bfloat16)


def body(nodes, grad_out, features, weight, tile_values, tile_rows, tile_cols, tile_count):
    tile = tile_values.shape[-1]
    width = grad_out.shape[1]
    cols = lax.axis_size(COL)
    share = width // cols
    gathered = lax.all_gather(grad_out, ROW, axis=0, tiled=True)
    own_features = lax.all_gather(features, COL, axis=0, tiled=True)
    smem, vmem = pl.BlockSpec(memory_space=pltpu.SMEM), pl.BlockSpec(memory_space=pltpu.VMEM)
    parts = pl.pallas_call(
        tiles_kernel,
        out_shape=jax.ShapeDtypeStruct((cols, tile + share, width), jnp.bfloat16),
        in_specs=[smem] * 3 + [vmem] * 3,
        out_specs=vmem,
        scratch_shapes=[pltpu.VMEM((cols, tile, width), jnp.float32)],
        compiler_params=pltpu.CompilerParams(vmem_limit_bytes=24 * 2**20),
    )(
        tile_count[0],
        tile_rows[0, 0],
        tile_cols[0, 0],
        tile_values[0, 0],
        gathered.reshape(-1, tile, width),
        own_features,
    )
    parts = lax.all_to_all(parts, COL, 0, 0, tiled=True)
    input_grad, grad_share = pl.pallas_call(
        functools.partial(finish_kernel, nodes**-0.5),
        out_shape=(
            jax.ShapeDtypeStruct((tile, width), jnp.bfloat16),
            jax.ShapeDtypeStruct((share, width), jnp.float32),
        ),
        in_specs=[vmem] * 2,
        out_specs=(vmem, vmem),
        compiler_params=pltpu.CompilerParams(vmem_limit_bytes=8 * 2**20),
    )(parts, weight)
    for axes in ("core", "zl", "zm", "zh"):
        grad_share = jnp.sum(lax.all_gather(grad_share, axes), axis=0)
    weight_grad = lax.all_gather(grad_share, COL, axis=0, tiled=True)
    return input_grad, weight_grad


def solution(mesh):
    fine = Mesh(mesh.devices.reshape(4, 4, 2, 2, 4, 4), ROW + COL)
    placed = (
        P(COL + ROW, None),
        P(ROW + COL, None),
        P(),
        P(ROW, COL, None, None, None),
        P(ROW, COL, None),
        P(ROW, COL, None),
        P(ROW, COL),
    )

    def whole(grad_out, *rest):
        return jax.shard_map(
            functools.partial(body, grad_out.shape[0]),
            mesh=fine,
            in_specs=placed,
            out_specs=(P(ROW + COL, None), P()),
            check_vma=False,
        )(grad_out, *rest)

    return whole
```

```python
import functools

import jax
import jax.numpy as jnp
from jax import lax
from jax.experimental import pallas as pl
from jax.experimental.pallas import tpu as pltpu
from jax.sharding import Mesh
from jax.sharding import PartitionSpec as P

Z = ("zh", "zm", "zl")
ROW = Z + ("core",)
COL = ("x", "y")


def tiles_kernel(count_ref, rows_ref, places_ref, values_ref, *refs):
    *pieces, features_ref, out_ref, values, gathered, total, copied = refs
    row_tiles, tile, width = total.shape
    share = features_ref.shape[1] // row_tiles
    copies = [pltpu.make_async_copy(values_ref, values, copied.at[0])]
    first = 0
    for index, piece in enumerate(pieces):
        place = gathered.at[first : first + piece.shape[0]]
        copies.append(pltpu.make_async_copy(piece, place, copied.at[index + 1]))
        first += piece.shape[0]
    for copy in copies:
        copy.start()
    total[...] = jnp.zeros_like(total)
    for copy in copies:
        copy.wait()

    def add(slot):
        row = rows_ref[slot]
        total[row] += jnp.dot(
            values[slot], gathered[places_ref[slot]], preferred_element_type=jnp.float32
        )

    count = count_ref[0]
    fours = lax.shift_right_logical(count, 2)

    def four(index, carry):
        for offset in range(4):
            add(4 * index + offset)
        return carry

    def one(slot, carry):
        add(slot)
        return carry

    lax.fori_loop(0, fours, four, 0)
    lax.fori_loop(4 * fours, count, one, 0)

    step = 4
    grad = jnp.zeros((features_ref.shape[1], width), jnp.float32)
    for first in range(0, row_tiles, step):
        part = total[first : first + step].astype(jnp.bfloat16)
        out_ref[first : first + step, :tile] = part
        grad += lax.dot_general(
            features_ref[first * tile : (first + step) * tile],
            part.reshape(step * tile, width),
            (((0,), (0,)), ((), ())),
            preferred_element_type=jnp.float32,
        )
    out_ref[:, tile:] = grad.astype(jnp.bfloat16).reshape(row_tiles, share, width)


def finish_kernel(scale, parts_ref, weight_ref, input_ref, share_ref):
    tile = input_ref.shape[0]
    summed = parts_ref[0].astype(jnp.float32)
    for other in range(1, parts_ref.shape[0]):
        summed += parts_ref[other].astype(jnp.float32)
    share_ref[...] = summed[tile:] * scale
    input_ref[...] = lax.dot_general(
        summed[:tile].astype(jnp.bfloat16),
        weight_ref[...],
        (((1,), (1,)), ((), ())),
        preferred_element_type=jnp.float32,
    ).astype(jnp.bfloat16)


def shifted(step):
    size = lax.axis_size(Z)
    return [(index, (index + step) % size) for index in range(size)]


def from_all(array, axes):
    size = lax.axis_size(axes)
    same = jnp.broadcast_to(array[None], (size, *array.shape))
    return lax.all_to_all(same, axes, 0, 0, tiled=True)


def gather_row(grad_out):
    own = lax.all_gather(grad_out, "zh")
    left, right = [own], [own]
    for unused in range(3):
        left.append(lax.ppermute(left[-1], Z, shifted(1)))
        right.append(lax.ppermute(right[-1], Z, shifted(-1)))
    far = lax.ppermute(left[3], Z, shifted(1))
    early = jnp.concatenate([own, left[1], right[1], left[2], right[2]])
    late = jnp.concatenate([left[3], right[3], far])
    swap = [(0, 1), (1, 0)]
    return early, late, lax.ppermute(early, "core", swap), lax.ppermute(late, "core", swap)


def place_of(block):
    high, residue, core = block >> 4, (block >> 1) & 7, block & 1
    away = (residue - (lax.axis_index("zm") * 2 + lax.axis_index("zl"))) & 7
    group = jnp.where(away < 4, 2 * away, jnp.where(away == 4, 7, 15 - 2 * away))
    return (core ^ lax.axis_index("core")) * 32 + group * 4 + high


def body(nodes, grad_out, features, weight, tile_values, tile_rows, tile_cols, tile_count):
    tile = tile_values.shape[-1]
    width = grad_out.shape[1]
    cols = lax.axis_size(COL)
    share = width // cols
    own_features = lax.all_gather(features, COL, axis=0, tiled=True)
    pieces = gather_row(grad_out)
    smem, vmem = pl.BlockSpec(memory_space=pltpu.SMEM), pl.BlockSpec(memory_space=pltpu.VMEM)
    anywhere = pl.BlockSpec(memory_space=pl.ANY)
    parts = pl.pallas_call(
        tiles_kernel,
        out_shape=jax.ShapeDtypeStruct((cols, tile + share, width), jnp.bfloat16),
        in_specs=[smem] * 3 + [anywhere] * (1 + len(pieces)) + [vmem],
        out_specs=vmem,
        scratch_shapes=[
            pltpu.VMEM(tile_values.shape[2:], jnp.bfloat16),
            pltpu.VMEM((lax.axis_size(ROW), tile, width), jnp.bfloat16),
            pltpu.VMEM((cols, tile, width), jnp.float32),
            pltpu.SemaphoreType.DMA((1 + len(pieces),)),
        ],
        compiler_params=pltpu.CompilerParams(vmem_limit_bytes=24 * 2**20),
    )(
        tile_count[0],
        tile_rows[0, 0],
        place_of(tile_cols[0, 0]),
        tile_values[0, 0],
        *pieces,
        own_features,
    )
    parts = lax.all_to_all(parts, COL, 0, 0, tiled=True)
    input_grad, grad_share = pl.pallas_call(
        functools.partial(finish_kernel, nodes**-0.5),
        out_shape=(
            jax.ShapeDtypeStruct((tile, width), jnp.bfloat16),
            jax.ShapeDtypeStruct((share, width), jnp.float32),
        ),
        in_specs=[vmem] * 2,
        out_specs=(vmem, vmem),
        compiler_params=pltpu.CompilerParams(vmem_limit_bytes=8 * 2**20),
    )(parts, weight)
    grad_share = jnp.sum(lax.all_gather(grad_share, "core"), axis=0)
    half = share // 2
    mine = lax.dynamic_slice_in_dim(grad_share, half * lax.axis_index("core"), half)
    mine = jnp.sum(from_all(mine.astype(jnp.bfloat16), Z).astype(jnp.float32), axis=0)
    grad_share = lax.all_gather(mine, "core", axis=0, tiled=True)
    weight_grad = from_all(grad_share, COL).reshape(width, width)
    return input_grad, weight_grad


def solution(mesh):
    fine = Mesh(mesh.devices.reshape(4, 4, 2, 2, 4, 4), ROW + COL)
    placed = (
        P(COL + ROW, None),
        P(ROW + COL, None),
        P(),
        P(ROW, COL, None, None, None),
        P(ROW, COL, None),
        P(ROW, COL, None),
        P(ROW, COL),
    )

    def whole(grad_out, *rest):
        return jax.shard_map(
            functools.partial(body, grad_out.shape[0]),
            mesh=fine,
            in_specs=placed,
            out_specs=(P(ROW + COL, None), P()),
            check_vma=False,
        )(grad_out, *rest)

    return whole
```

```python
import functools

import jax
import jax.numpy as jnp
from jax import lax
from jax.experimental import pallas as pl
from jax.experimental.pallas import tpu as pltpu
from jax.sharding import Mesh
from jax.sharding import PartitionSpec as P

Z = ("zh", "zm", "zl")
ROW = Z + ("core",)
COL = ("x", "y")


def tiles_kernel(count_ref, rows_ref, places_ref, values_ref, *refs):
    *pieces, features_ref, out_ref, share_ref, values, gathered, total, copied = refs
    row_tiles, tile, width = total.shape
    share = features_ref.shape[1] // row_tiles
    copies = [pltpu.make_async_copy(values_ref, values, copied.at[0])]
    first = 0
    for index, piece in enumerate(pieces):
        place = gathered.at[first : first + piece.shape[0]]
        copies.append(pltpu.make_async_copy(piece, place, copied.at[index + 1]))
        first += piece.shape[0]
    for copy in copies:
        copy.start()
    total[...] = jnp.zeros_like(total)
    for copy in copies:
        copy.wait()

    def add(slot):
        row = rows_ref[slot]
        total[row] += jnp.dot(
            values[slot], gathered[places_ref[slot]], preferred_element_type=jnp.float32
        )

    count = count_ref[0]
    fours = lax.shift_right_logical(count, 2)

    def four(index, carry):
        for offset in range(4):
            add(4 * index + offset)
        return carry

    def one(slot, carry):
        add(slot)
        return carry

    lax.fori_loop(0, fours, four, 0)
    lax.fori_loop(4 * fours, count, one, 0)

    step = 4
    grad = jnp.zeros((features_ref.shape[1], width), jnp.float32)
    for first in range(0, row_tiles, step):
        part = total[first : first + step].astype(jnp.bfloat16)
        out_ref[first : first + step] = part
        grad += lax.dot_general(
            features_ref[first * tile : (first + step) * tile],
            part.reshape(step * tile, width),
            (((0,), (0,)), ((), ())),
            preferred_element_type=jnp.float32,
        )
    share_ref[...] = grad.astype(jnp.bfloat16).reshape(row_tiles, share, width)


def sum_of(parts_ref):
    summed = parts_ref[0].astype(jnp.float32)
    for other in range(1, parts_ref.shape[0]):
        summed += parts_ref[other].astype(jnp.float32)
    return summed


def share_kernel(scale, shares_ref, parts_ref, share_ref, same_parts_ref):
    share_ref[...] = sum_of(shares_ref) * scale


def finish_kernel(parts_ref, weight_ref, input_ref):
    input_ref[...] = lax.dot_general(
        sum_of(parts_ref).astype(jnp.bfloat16),
        weight_ref[...],
        (((1,), (1,)), ((), ())),
        preferred_element_type=jnp.float32,
    ).astype(jnp.bfloat16)


def shifted(step):
    size = lax.axis_size(Z)
    return [(index, (index + step) % size) for index in range(size)]


def from_all(array, axes):
    size = lax.axis_size(axes)
    same = jnp.broadcast_to(array[None], (size, *array.shape))
    return lax.all_to_all(same, axes, 0, 0, tiled=True)


def gather_row(grad_out, beside):
    own, beside = lax.optimization_barrier((lax.all_gather(grad_out, "zh"), beside))
    left, right = [own], [own]
    for unused in range(3):
        left.append(lax.ppermute(left[-1], Z, shifted(1)))
        right.append(lax.ppermute(right[-1], Z, shifted(-1)))
    crossed = [(2 * source + core, 2 * target + 1 - core) for source, target in shifted(1) for core in (0, 1)]
    far, far_other = lax.ppermute(left[3], Z, shifted(1)), lax.ppermute(left[3], ROW, crossed)
    early = jnp.concatenate([own, left[1], right[1], left[2], right[2]])
    late = jnp.concatenate([left[3], right[3]])
    swap = [(0, 1), (1, 0)]
    return early, late, far, lax.ppermute(early, "core", swap), lax.ppermute(late, "core", swap), far_other, beside


def place_of(block):
    high, residue, core = block >> 4, (block >> 1) & 7, block & 1
    away = (residue - (lax.axis_index("zm") * 2 + lax.axis_index("zl"))) & 7
    group = jnp.where(away < 4, 2 * away, jnp.where(away == 4, 7, 15 - 2 * away))
    return (core ^ lax.axis_index("core")) * 32 + group * 4 + high


def body(nodes, grad_out, features, weight, tile_values, tile_rows, tile_cols, tile_count):
    tile = tile_values.shape[-1]
    width = grad_out.shape[1]
    cols = lax.axis_size(COL)
    share = width // cols
    own_features = from_all(features, COL).reshape(-1, width)
    *pieces, own_features = gather_row(grad_out, own_features)
    smem, vmem = pl.BlockSpec(memory_space=pltpu.SMEM), pl.BlockSpec(memory_space=pltpu.VMEM)
    anywhere = pl.BlockSpec(memory_space=pl.ANY)
    parts, shares = pl.pallas_call(
        tiles_kernel,
        out_shape=(
            jax.ShapeDtypeStruct((cols, tile, width), jnp.bfloat16),
            jax.ShapeDtypeStruct((cols, share, width), jnp.bfloat16),
        ),
        in_specs=[smem] * 3 + [anywhere] * (1 + len(pieces)) + [vmem],
        out_specs=(vmem, vmem),
        scratch_shapes=[
            pltpu.VMEM(tile_values.shape[2:], jnp.bfloat16),
            pltpu.VMEM((lax.axis_size(ROW), tile, width), jnp.bfloat16),
            pltpu.VMEM((cols, tile, width), jnp.float32),
            pltpu.SemaphoreType.DMA((1 + len(pieces),)),
        ],
        compiler_params=pltpu.CompilerParams(vmem_limit_bytes=24 * 2**20),
    )(
        tile_count[0],
        tile_rows[0, 0],
        place_of(tile_cols[0, 0]),
        tile_values[0, 0],
        *pieces,
        own_features,
    )
    shares = lax.all_to_all(shares, COL, 0, 0, tiled=True)
    grad_share, parts = pl.pallas_call(
        functools.partial(share_kernel, nodes**-0.5),
        out_shape=(
            jax.ShapeDtypeStruct((share, width), jnp.float32),
            jax.ShapeDtypeStruct(parts.shape, parts.dtype),
        ),
        in_specs=[vmem, anywhere],
        out_specs=(vmem, anywhere),
        input_output_aliases={1: 1},
        compiler_params=pltpu.CompilerParams(vmem_limit_bytes=4 * 2**20),
    )(shares, parts)
    parts = lax.all_to_all(parts, COL, 0, 0, tiled=True)
    grad_share = jnp.sum(lax.all_gather(grad_share, "core"), axis=0)
    half = share // 2
    mine = lax.dynamic_slice_in_dim(grad_share, half * lax.axis_index("core"), half)
    mine = lax.all_gather(mine.astype(jnp.bfloat16), Z)
    mine, parts = lax.optimization_barrier((mine, parts))
    mine = jnp.sum(mine.astype(jnp.float32), axis=0)
    grad_share = lax.all_gather(mine, "core", axis=0, tiled=True)
    weight_grad = from_all(grad_share, COL).reshape(width, width)
    input_grad = pl.pallas_call(
        finish_kernel,
        out_shape=jax.ShapeDtypeStruct((tile, width), jnp.bfloat16),
        in_specs=[vmem] * 2,
        out_specs=vmem,
        compiler_params=pltpu.CompilerParams(vmem_limit_bytes=8 * 2**20),
    )(parts, weight)
    return input_grad, weight_grad


def solution(mesh):
    fine = Mesh(mesh.devices.reshape(4, 4, 2, 2, 4, 4), ROW + COL)
    placed = (
        P(COL + ROW, None),
        P(ROW + COL, None),
        P(),
        P(ROW, COL, None, None, None),
        P(ROW, COL, None),
        P(ROW, COL, None),
        P(ROW, COL),
    )

    def whole(grad_out, *rest):
        return jax.shard_map(
            functools.partial(body, grad_out.shape[0]),
            mesh=fine,
            in_specs=placed,
            out_specs=(P(ROW + COL, None), P()),
            check_vma=False,
        )(grad_out, *rest)

    return whole
```

```python
import functools

import jax
import jax.numpy as jnp
from jax import lax
from jax.experimental import pallas as pl
from jax.experimental.pallas import tpu as pltpu
from jax.sharding import Mesh
from jax.sharding import PartitionSpec as P

Z = ("za", "zb")
ROW = Z + ("core",)
COL = ("x", "y")


def tiles_kernel(count_ref, rows_ref, places_ref, values_ref, *refs):
    *pieces, features_ref, out_ref, share_ref, gathered, total, copied = refs
    row_tiles, tile, width = total.shape
    share = features_ref.shape[1] // row_tiles
    copies, first = [], 0
    for index, piece in enumerate(pieces):
        place = gathered.at[first : first + piece.shape[0]]
        copies.append(pltpu.make_async_copy(piece, place, copied.at[index]))
        first += piece.shape[0]
    for copy in copies:
        copy.start()
    total[...] = jnp.zeros_like(total)
    for copy in copies:
        copy.wait()

    def add(slot):
        row = rows_ref[slot]
        total[row] += jnp.dot(
            values_ref[slot], gathered[places_ref[slot]], preferred_element_type=jnp.float32
        )

    count = count_ref[0]
    fours = lax.shift_right_logical(count, 2)

    def four(index, carry):
        for offset in range(4):
            add(4 * index + offset)
        return carry

    def one(slot, carry):
        add(slot)
        return carry

    lax.fori_loop(0, fours, four, 0)
    lax.fori_loop(4 * fours, count, one, 0)

    step = 4
    grad = jnp.zeros((features_ref.shape[1], width), jnp.float32)
    for first in range(0, row_tiles, step):
        part = total[first : first + step].astype(jnp.bfloat16)
        out_ref[first : first + step] = part
        grad += lax.dot_general(
            features_ref[first * tile : (first + step) * tile],
            part.reshape(step * tile, width),
            (((0,), (0,)), ((), ())),
            preferred_element_type=jnp.float32,
        )
    share_ref[...] = grad.astype(jnp.bfloat16).reshape(row_tiles, share, width)


def sum_of(parts_ref):
    summed = parts_ref[0].astype(jnp.float32)
    for other in range(1, parts_ref.shape[0]):
        summed += parts_ref[other].astype(jnp.float32)
    return summed


def share_kernel(scale, shares_ref, parts_ref, share_ref, same_parts_ref):
    share_ref[...] = sum_of(shares_ref) * scale


def finish_kernel(parts_ref, weight_ref, input_ref):
    input_ref[...] = lax.dot_general(
        sum_of(parts_ref).astype(jnp.bfloat16),
        weight_ref[...],
        (((1,), (1,)), ((), ())),
        preferred_element_type=jnp.float32,
    ).astype(jnp.bfloat16)


def shifted(step):
    size = lax.axis_size(Z)
    return [(index, (index + step) % size) for index in range(size)]


def from_all(array, axes):
    size = lax.axis_size(axes)
    same = jnp.broadcast_to(array[None], (size, *array.shape))
    return lax.all_to_all(same, axes, 0, 0, tiled=True)


def gather_row(grad_out, beside):
    own, beside = lax.optimization_barrier((lax.all_gather(grad_out, "za"), beside))
    left, right = lax.ppermute(own, Z, shifted(1)), lax.ppermute(own, Z, shifted(-1))
    half = own.shape[0] // 2
    pieces = [own, left, right]
    others = [lax.ppermute(piece, "core", [(0, 1), (1, 0)]) for piece in pieces]
    for block, step in ((left[:half], 1), (right[half:], -1)):
        crossed = [
            (2 * source + core, 2 * target + 1 - core) for source, target in shifted(step) for core in (0, 1)
        ]
        pieces.append(lax.ppermute(block, Z, shifted(step)))
        others.append(lax.ppermute(block, ROW, crossed))
    return *pieces, *others, beside


def place_of(block):
    high, residue, core = block >> 3, (block >> 1) & 3, block & 1
    away = (residue - lax.axis_index("zb")) & 3
    group = jnp.where(away == 3, 1, jnp.where(away == 0, 0, away + 1))
    return (core ^ lax.axis_index("core")) * 32 + group * 8 + high


def body(nodes, grad_out, features, weight, tile_values, tile_rows, tile_cols, tile_count):
    tile = tile_values.shape[-1]
    width = grad_out.shape[1]
    cols = lax.axis_size(COL)
    share = width // cols
    own_features = from_all(features, COL).reshape(-1, width)
    *pieces, own_features = gather_row(grad_out, own_features)
    smem, vmem = pl.BlockSpec(memory_space=pltpu.SMEM), pl.BlockSpec(memory_space=pltpu.VMEM)
    anywhere = pl.BlockSpec(memory_space=pl.ANY)
    parts, shares = pl.pallas_call(
        tiles_kernel,
        out_shape=(
            jax.ShapeDtypeStruct((cols, tile, width), jnp.bfloat16),
            jax.ShapeDtypeStruct((cols, share, width), jnp.bfloat16),
        ),
        in_specs=[smem] * 3 + [vmem] + [anywhere] * len(pieces) + [vmem],
        out_specs=(vmem, vmem),
        scratch_shapes=[
            pltpu.VMEM((lax.axis_size(ROW), tile, width), jnp.bfloat16),
            pltpu.VMEM((cols, tile, width), jnp.float32),
            pltpu.SemaphoreType.DMA((len(pieces),)),
        ],
        compiler_params=pltpu.CompilerParams(vmem_limit_bytes=24 * 2**20),
    )(
        tile_count[0],
        tile_rows[0, 0],
        place_of(tile_cols[0, 0]),
        tile_values[0, 0],
        *pieces,
        own_features,
    )
    shares = lax.all_to_all(shares, COL, 0, 0, tiled=True)
    grad_share, parts = pl.pallas_call(
        functools.partial(share_kernel, nodes**-0.5),
        out_shape=(
            jax.ShapeDtypeStruct((share, width), jnp.float32),
            jax.ShapeDtypeStruct(parts.shape, parts.dtype),
        ),
        in_specs=[vmem, anywhere],
        out_specs=(vmem, anywhere),
        input_output_aliases={1: 1},
        compiler_params=pltpu.CompilerParams(vmem_limit_bytes=4 * 2**20),
    )(shares, parts)
    parts = lax.all_to_all(parts, COL, 0, 0, tiled=True)
    grad_share = jnp.sum(lax.all_gather(grad_share, "core"), axis=0)
    half = share // 2
    mine = lax.dynamic_slice_in_dim(grad_share, half * lax.axis_index("core"), half)
    mine = lax.all_gather(mine.astype(jnp.bfloat16), Z)
    mine, parts = lax.optimization_barrier((mine, parts))
    mine = jnp.sum(mine.astype(jnp.float32), axis=0)
    grad_share = lax.all_gather(mine, "core", axis=0, tiled=True)
    weight_grad = from_all(grad_share, COL).reshape(width, width)
    input_grad = pl.pallas_call(
        finish_kernel,
        out_shape=jax.ShapeDtypeStruct((tile, width), jnp.bfloat16),
        in_specs=[vmem] * 2,
        out_specs=vmem,
        compiler_params=pltpu.CompilerParams(vmem_limit_bytes=8 * 2**20),
    )(parts, weight)
    return input_grad, weight_grad


def solution(mesh):
    fine = Mesh(mesh.devices.reshape(8, 4, 2, 4, 4), ROW + COL)
    placed = (
        P(COL + ROW, None),
        P(ROW + COL, None),
        P(),
        P(ROW, COL, None, None, None),
        P(ROW, COL, None),
        P(ROW, COL, None),
        P(ROW, COL),
    )

    def whole(grad_out, *rest):
        return jax.shard_map(
            functools.partial(body, grad_out.shape[0]),
            mesh=fine,
            in_specs=placed,
            out_specs=(P(ROW + COL, None), P()),
            check_vma=False,
        )(grad_out, *rest)

    return whole
```

```python
import functools

import jax
import jax.numpy as jnp
from jax import lax
from jax.experimental import pallas as pl
from jax.experimental.pallas import tpu as pltpu
from jax.sharding import Mesh
from jax.sharding import PartitionSpec as P

Z = ("za", "zb")
ROW = Z + ("core",)
COL = ("x", "y")


def tiles_kernel(count_ref, rows_ref, places_ref, values_ref, *refs):
    *pieces, features_ref, out_ref, share_ref, gathered, total, copied = refs
    row_tiles, tile, width = total.shape
    share = features_ref.shape[1] // row_tiles
    copies, first = [], 0
    for index, piece in enumerate(pieces):
        place = gathered.at[first : first + piece.shape[0]]
        copies.append(pltpu.make_async_copy(piece, place, copied.at[index]))
        first += piece.shape[0]
    for copy in copies:
        copy.start()
    total[...] = jnp.zeros_like(total)
    for copy in copies:
        copy.wait()

    def add(slot):
        row = rows_ref[slot]
        total[row] += jnp.dot(
            values_ref[slot], gathered[places_ref[slot]], preferred_element_type=jnp.float32
        )

    count = count_ref[0]
    fours = lax.shift_right_logical(count, 2)

    def four(index, carry):
        for offset in range(4):
            add(4 * index + offset)
        return carry

    def one(slot, carry):
        add(slot)
        return carry

    lax.fori_loop(0, fours, four, 0)
    lax.fori_loop(4 * fours, count, one, 0)

    step = 4
    grad = jnp.zeros((features_ref.shape[1], width), jnp.float32)
    for first in range(0, row_tiles, step):
        part = total[first : first + step].astype(jnp.bfloat16)
        out_ref[first : first + step] = part
        grad += lax.dot_general(
            features_ref[first * tile : (first + step) * tile],
            part.reshape(step * tile, width),
            (((0,), (0,)), ((), ())),
            preferred_element_type=jnp.float32,
        )
    share_ref[...] = grad.astype(jnp.bfloat16).reshape(row_tiles, share, width)


def sum_of(parts_ref):
    summed = parts_ref[0].astype(jnp.float32)
    for other in range(1, parts_ref.shape[0]):
        summed += parts_ref[other].astype(jnp.float32)
    return summed


def share_kernel(scale, shares_ref, share_ref):
    share_ref[...] = sum_of(shares_ref) * scale


def finish_kernel(parts_ref, weight_ref, input_ref):
    input_ref[...] = lax.dot_general(
        sum_of(parts_ref).astype(jnp.bfloat16),
        weight_ref[...],
        (((1,), (1,)), ((), ())),
        preferred_element_type=jnp.float32,
    ).astype(jnp.bfloat16)


def shifted(step):
    size = lax.axis_size(Z)
    return [(index, (index + step) % size) for index in range(size)]


def from_all(array, axes):
    size = lax.axis_size(axes)
    same = jnp.broadcast_to(array[None], (size, *array.shape))
    return lax.all_to_all(same, axes, 0, 0, tiled=True)


def gather_row(grad_out, beside):
    own, beside = lax.optimization_barrier((lax.all_gather(grad_out, "za"), beside))
    half = own.shape[0] // 2
    pieces = [own]
    for block, step in ((own, 1), (own, -1), (own[:half], 2), (own[half:], -2)):
        pieces.append(lax.ppermute(block, Z, shifted(step)))
    others = [lax.ppermute(piece, "core", [(0, 1), (1, 0)]) for piece in pieces]
    return *pieces, *others, beside


def place_of(block):
    high, residue, core = block >> 3, (block >> 1) & 3, block & 1
    away = (residue - lax.axis_index("zb")) & 3
    group = jnp.where(away == 3, 1, jnp.where(away == 0, 0, away + 1))
    return (core ^ lax.axis_index("core")) * 32 + group * 8 + high


def body(nodes, grad_out, features, weight, tile_values, tile_rows, tile_cols, tile_count):
    tile = tile_values.shape[-1]
    width = grad_out.shape[1]
    cols = lax.axis_size(COL)
    share = width // cols
    own_features = from_all(features, COL).reshape(-1, width)
    *pieces, own_features = gather_row(grad_out, own_features)
    smem, vmem = pl.BlockSpec(memory_space=pltpu.SMEM), pl.BlockSpec(memory_space=pltpu.VMEM)
    anywhere = pl.BlockSpec(memory_space=pl.ANY)
    parts, shares = pl.pallas_call(
        tiles_kernel,
        out_shape=(
            jax.ShapeDtypeStruct((cols, tile, width), jnp.bfloat16),
            jax.ShapeDtypeStruct((cols, share, width), jnp.bfloat16),
        ),
        in_specs=[smem] * 3 + [vmem] + [anywhere] * len(pieces) + [vmem],
        out_specs=(vmem, vmem),
        scratch_shapes=[
            pltpu.VMEM((lax.axis_size(ROW), tile, width), jnp.bfloat16),
            pltpu.VMEM((cols, tile, width), jnp.float32),
            pltpu.SemaphoreType.DMA((len(pieces),)),
        ],
        compiler_params=pltpu.CompilerParams(vmem_limit_bytes=24 * 2**20),
    )(
        tile_count[0],
        tile_rows[0, 0],
        place_of(tile_cols[0, 0]),
        tile_values[0, 0],
        *pieces,
        own_features,
    )
    shares = lax.all_to_all(shares, COL, 0, 0, tiled=True)
    grad_share = pl.pallas_call(
        functools.partial(share_kernel, nodes**-0.5),
        out_shape=jax.ShapeDtypeStruct((share, width), jnp.float32),
        in_specs=[vmem],
        out_specs=vmem,
        compiler_params=pltpu.CompilerParams(vmem_limit_bytes=4 * 2**20),
    )(shares)
    grad_share = jnp.sum(from_all(grad_share, ("zb", "core")), axis=0)
    half = share // 2
    mine = lax.dynamic_slice_in_dim(grad_share, half * lax.axis_index("core"), half).astype(jnp.bfloat16)
    mine, parts = lax.optimization_barrier((mine, parts))
    parts = lax.all_to_all(parts, COL, 0, 0, tiled=True)
    mine = lax.all_gather(mine, "za")
    mine, parts = lax.optimization_barrier((mine, parts))
    mine = jnp.sum(mine.astype(jnp.float32), axis=0)
    grad_share = lax.all_gather(mine, "core", axis=0, tiled=True)
    weight_grad = from_all(grad_share, COL).reshape(width, width)
    input_grad = pl.pallas_call(
        finish_kernel,
        out_shape=jax.ShapeDtypeStruct((tile, width), jnp.bfloat16),
        in_specs=[vmem] * 2,
        out_specs=vmem,
        compiler_params=pltpu.CompilerParams(vmem_limit_bytes=8 * 2**20),
    )(parts, weight)
    return input_grad, weight_grad


def solution(mesh):
    fine = Mesh(mesh.devices.reshape(8, 4, 2, 4, 4), ROW + COL)
    placed = (
        P(COL + ROW, None),
        P(ROW + COL, None),
        P(),
        P(ROW, COL, None, None, None),
        P(ROW, COL, None),
        P(ROW, COL, None),
        P(ROW, COL),
    )

    def whole(grad_out, *rest):
        return jax.shard_map(
            functools.partial(body, grad_out.shape[0]),
            mesh=fine,
            in_specs=placed,
            out_specs=(P(ROW + COL, None), P()),
            check_vma=False,
        )(grad_out, *rest)

    return whole
```

```python
import functools

import jax
import jax.numpy as jnp
from jax import lax
from jax.experimental import pallas as pl
from jax.experimental.pallas import tpu as pltpu
from jax.sharding import Mesh
from jax.sharding import PartitionSpec as P

Z = ("za", "zb")
ROW = Z + ("core",)
COL = ("x", "y")


def tiles_kernel(count_ref, rows_ref, places_ref, values_ref, *refs):
    *pieces, features_ref, out_ref, share_ref, gathered, total, copied = refs
    row_tiles, tile, width = total.shape
    share = features_ref.shape[1] // row_tiles
    copies, first = [], 0
    for index, piece in enumerate(pieces):
        place = gathered.at[first : first + piece.shape[0]]
        copies.append(pltpu.make_async_copy(piece, place, copied.at[index]))
        first += piece.shape[0]
    for copy in copies:
        copy.start()
    total[...] = jnp.zeros_like(total)
    for copy in copies:
        copy.wait()

    def add(slot):
        row = rows_ref[slot]
        total[row] += jnp.dot(
            values_ref[slot], gathered[places_ref[slot]], preferred_element_type=jnp.float32
        )

    count = count_ref[0]
    fours = lax.shift_right_logical(count, 2)

    def four(index, carry):
        for offset in range(4):
            add(4 * index + offset)
        return carry

    def one(slot, carry):
        add(slot)
        return carry

    lax.fori_loop(0, fours, four, 0)
    lax.fori_loop(4 * fours, count, one, 0)

    step = 4
    grad = jnp.zeros((features_ref.shape[1], width), jnp.float32)
    for first in range(0, row_tiles, step):
        part = total[first : first + step].astype(jnp.bfloat16)
        out_ref[first : first + step] = part
        grad += lax.dot_general(
            features_ref[first * tile : (first + step) * tile],
            part.reshape(step * tile, width),
            (((0,), (0,)), ((), ())),
            preferred_element_type=jnp.float32,
        )
    share_ref[...] = grad.astype(jnp.bfloat16).reshape(row_tiles, share, width)


def sum_of(parts_ref):
    summed = parts_ref[0].astype(jnp.float32)
    for other in range(1, parts_ref.shape[0]):
        summed += parts_ref[other].astype(jnp.float32)
    return summed


def share_kernel(scale, shares_ref, share_ref):
    share_ref[...] = sum_of(shares_ref) * scale


def finish_kernel(parts_ref, weight_ref, input_ref):
    input_ref[...] = lax.dot_general(
        sum_of(parts_ref).astype(jnp.bfloat16),
        weight_ref[...],
        (((1,), (1,)), ((), ())),
        preferred_element_type=jnp.float32,
    ).astype(jnp.bfloat16)


def shifted(step):
    size = lax.axis_size(Z)
    return [(index, (index + step) % size) for index in range(size)]


def from_all(array, axes):
    size = lax.axis_size(axes)
    same = jnp.broadcast_to(array[None], (size, *array.shape))
    return lax.all_to_all(same, axes, 0, 0, tiled=True)


def gather_row(grad_out, beside):
    own, beside = lax.optimization_barrier((lax.all_gather(grad_out, "za"), beside))
    half = own.shape[0] // 2
    pieces = [own]
    for block, step in ((own, 1), (own, -1), (own[:half], 2), (own[half:], -2)):
        pieces.append(lax.ppermute(block, Z, shifted(step)))
    swap = [(0, 1), (1, 0)]
    first, unused = lax.optimization_barrier((own, pieces[2]))
    others = [lax.ppermute(piece, "core", swap) for piece in (first, *pieces[1:])]
    return *pieces, *others, beside


def place_of(block):
    high, residue, core = block >> 3, (block >> 1) & 3, block & 1
    away = (residue - lax.axis_index("zb")) & 3
    group = jnp.where(away == 3, 1, jnp.where(away == 0, 0, away + 1))
    return (core ^ lax.axis_index("core")) * 32 + group * 8 + high


def body(nodes, grad_out, features, weight, tile_values, tile_rows, tile_cols, tile_count):
    tile = tile_values.shape[-1]
    width = grad_out.shape[1]
    cols = lax.axis_size(COL)
    share = width // cols
    own_features = from_all(features, COL).reshape(-1, width)
    *pieces, own_features = gather_row(grad_out, own_features)
    smem, vmem = pl.BlockSpec(memory_space=pltpu.SMEM), pl.BlockSpec(memory_space=pltpu.VMEM)
    anywhere = pl.BlockSpec(memory_space=pl.ANY)
    parts, shares = pl.pallas_call(
        tiles_kernel,
        out_shape=(
            jax.ShapeDtypeStruct((cols, tile, width), jnp.bfloat16),
            jax.ShapeDtypeStruct((cols, share, width), jnp.bfloat16),
        ),
        in_specs=[smem] * 3 + [vmem] + [anywhere] * len(pieces) + [vmem],
        out_specs=(vmem, vmem),
        scratch_shapes=[
            pltpu.VMEM((lax.axis_size(ROW), tile, width), jnp.bfloat16),
            pltpu.VMEM((cols, tile, width), jnp.float32),
            pltpu.SemaphoreType.DMA((len(pieces),)),
        ],
        compiler_params=pltpu.CompilerParams(vmem_limit_bytes=24 * 2**20),
    )(
        tile_count[0],
        tile_rows[0, 0],
        place_of(tile_cols[0, 0]),
        tile_values[0, 0],
        *pieces,
        own_features,
    )
    shares = lax.all_to_all(shares, COL, 0, 0, tiled=True)
    grad_share = pl.pallas_call(
        functools.partial(share_kernel, nodes**-0.5),
        out_shape=jax.ShapeDtypeStruct((share, width), jnp.float32),
        in_specs=[vmem],
        out_specs=vmem,
        compiler_params=pltpu.CompilerParams(vmem_limit_bytes=4 * 2**20),
    )(shares)
    grad_share = jnp.sum(from_all(grad_share, ("zb", "core")), axis=0)
    grad_share, parts = lax.optimization_barrier((grad_share, parts))
    parts = lax.all_to_all(parts, COL, 0, 0, tiled=True)
    grad_share, parts = lax.optimization_barrier((lax.all_gather(grad_share, "za"), parts))
    grad_share = jnp.sum(grad_share, axis=0).astype(jnp.bfloat16)
    weight_grad = from_all(grad_share, COL).reshape(width, width).astype(jnp.float32)
    input_grad = pl.pallas_call(
        finish_kernel,
        out_shape=jax.ShapeDtypeStruct((tile, width), jnp.bfloat16),
        in_specs=[vmem] * 2,
        out_specs=vmem,
        compiler_params=pltpu.CompilerParams(vmem_limit_bytes=8 * 2**20),
    )(parts, weight)
    return input_grad, weight_grad


def solution(mesh):
    fine = Mesh(mesh.devices.reshape(8, 4, 2, 4, 4), ROW + COL)
    placed = (
        P(COL + ROW, None),
        P(ROW + COL, None),
        P(),
        P(ROW, COL, None, None, None),
        P(ROW, COL, None),
        P(ROW, COL, None),
        P(ROW, COL),
    )

    def whole(grad_out, *rest):
        return jax.shard_map(
            functools.partial(body, grad_out.shape[0]),
            mesh=fine,
            in_specs=placed,
            out_specs=(P(ROW + COL, None), P()),
            check_vma=False,
        )(grad_out, *rest)

    return whole
```

```python
import functools

import jax
import jax.numpy as jnp
from jax import lax
from jax.experimental import pallas as pl
from jax.experimental.pallas import tpu as pltpu
from jax.sharding import Mesh
from jax.sharding import PartitionSpec as P

Z = ("za", "zb")
ROW = Z + ("core",)
COL = ("x", "y")
SHARE = ("core", "y")


def tiles_kernel(count_ref, rows_ref, places_ref, values_ref, *refs):
    *pieces, features_ref, out_ref, share_ref, gathered, total, copied = refs
    row_tiles, tile, width = total.shape
    copies, first = [], 0
    for index, piece in enumerate(pieces):
        place = gathered.at[first : first + piece.shape[0]]
        copies.append(pltpu.make_async_copy(piece, place, copied.at[index]))
        first += piece.shape[0]
    for copy in copies:
        copy.start()
    total[...] = jnp.zeros_like(total)
    for copy in copies:
        copy.wait()

    def add(slot):
        row = rows_ref[slot]
        total[row] += jnp.dot(
            values_ref[slot], gathered[places_ref[slot]], preferred_element_type=jnp.float32
        )

    count = count_ref[0]
    fours = lax.shift_right_logical(count, 2)

    def four(index, carry):
        for offset in range(4):
            add(4 * index + offset)
        return carry

    def one(slot, carry):
        add(slot)
        return carry

    lax.fori_loop(0, fours, four, 0)
    lax.fori_loop(4 * fours, count, one, 0)

    step = 4
    grad = jnp.zeros((features_ref.shape[1], width), jnp.float32)
    for first in range(0, row_tiles, step):
        part = total[first : first + step].astype(jnp.bfloat16)
        out_ref[first : first + step] = part
        grad += lax.dot_general(
            features_ref[first * tile : (first + step) * tile],
            part.reshape(step * tile, width),
            (((0,), (0,)), ((), ())),
            preferred_element_type=jnp.float32,
        )
    share_ref[...] = grad.astype(jnp.bfloat16).reshape(share_ref.shape)


def sum_of(parts_ref):
    summed = parts_ref[0].astype(jnp.float32)
    for other in range(1, parts_ref.shape[0]):
        summed += parts_ref[other].astype(jnp.float32)
    return summed


def share_kernel(scale, shares_ref, share_ref):
    share_ref[...] = sum_of(shares_ref) * scale


def finish_kernel(parts_ref, weight_ref, input_ref):
    input_ref[...] = lax.dot_general(
        sum_of(parts_ref).astype(jnp.bfloat16),
        weight_ref[...],
        (((1,), (1,)), ((), ())),
        preferred_element_type=jnp.float32,
    ).astype(jnp.bfloat16)


def shifted(step):
    size = lax.axis_size(Z)
    return [(index, (index + step) % size) for index in range(size)]


def from_all(array, axes):
    size = lax.axis_size(axes)
    same = jnp.broadcast_to(array[None], (size, *array.shape))
    return lax.all_to_all(same, axes, 0, 0, tiled=True)


def gather_row(grad_out, beside):
    own, beside = lax.optimization_barrier((lax.all_gather(grad_out, "za"), beside))
    half = own.shape[0] // 2
    left, right = lax.ppermute(own, Z, shifted(1)), lax.ppermute(own, Z, shifted(-1))
    low, high = lax.ppermute(left[:half], Z, shifted(1)), lax.ppermute(right[half:], Z, shifted(-1))
    pieces = [own, left, right, low, high]
    others = [lax.ppermute(piece, "core", [(0, 1), (1, 0)]) for piece in pieces]
    return *pieces, *others, beside


def place_of(block):
    high, residue, core = block >> 3, (block >> 1) & 3, block & 1
    away = (residue - lax.axis_index("zb")) & 3
    group = jnp.where(away == 3, 1, jnp.where(away == 0, 0, away + 1))
    return (core ^ lax.axis_index("core")) * 32 + group * 8 + high


def body(nodes, grad_out, features, weight, tile_values, tile_rows, tile_cols, tile_count):
    tile = tile_values.shape[-1]
    width = grad_out.shape[1]
    cols = lax.axis_size(COL)
    sharers = lax.axis_size(SHARE)
    share = width // sharers
    own_features = from_all(features, COL).reshape(-1, width)
    *pieces, own_features = gather_row(grad_out, own_features)
    smem, vmem = pl.BlockSpec(memory_space=pltpu.SMEM), pl.BlockSpec(memory_space=pltpu.VMEM)
    anywhere = pl.BlockSpec(memory_space=pl.ANY)
    parts, shares = pl.pallas_call(
        tiles_kernel,
        out_shape=(
            jax.ShapeDtypeStruct((cols, tile, width), jnp.bfloat16),
            jax.ShapeDtypeStruct((sharers, share, width), jnp.bfloat16),
        ),
        in_specs=[smem] * 3 + [vmem] + [anywhere] * len(pieces) + [vmem],
        out_specs=(vmem, vmem),
        scratch_shapes=[
            pltpu.VMEM((lax.axis_size(ROW), tile, width), jnp.bfloat16),
            pltpu.VMEM((cols, tile, width), jnp.float32),
            pltpu.SemaphoreType.DMA((len(pieces),)),
        ],
        compiler_params=pltpu.CompilerParams(vmem_limit_bytes=24 * 2**20),
    )(
        tile_count[0],
        tile_rows[0, 0],
        place_of(tile_cols[0, 0]),
        tile_values[0, 0],
        *pieces,
        own_features,
    )
    shares = lax.all_to_all(shares, SHARE, 0, 0, tiled=True)
    grad_share = pl.pallas_call(
        functools.partial(share_kernel, nodes**-0.5),
        out_shape=jax.ShapeDtypeStruct((share, width), jnp.float32),
        in_specs=[vmem],
        out_specs=vmem,
        compiler_params=pltpu.CompilerParams(vmem_limit_bytes=4 * 2**20),
    )(shares)
    grad_share = jnp.sum(from_all(grad_share, ("zb", "x")), axis=0)
    grad_share, parts = lax.optimization_barrier((grad_share, parts))
    parts = lax.all_to_all(parts, COL, 0, 0, tiled=True)
    grad_share, parts = lax.optimization_barrier((lax.all_gather(grad_share, "za"), parts))
    grad_share = jnp.sum(grad_share, axis=0).astype(jnp.bfloat16)
    weight_grad = from_all(grad_share, SHARE).reshape(width, width).astype(jnp.float32)
    input_grad = pl.pallas_call(
        finish_kernel,
        out_shape=jax.ShapeDtypeStruct((tile, width), jnp.bfloat16),
        in_specs=[vmem] * 2,
        out_specs=vmem,
        compiler_params=pltpu.CompilerParams(vmem_limit_bytes=8 * 2**20),
    )(parts, weight)
    return input_grad, weight_grad


def solution(mesh):
    fine = Mesh(mesh.devices.reshape(8, 4, 2, 4, 4), ROW + COL)
    placed = (
        P(COL + ROW, None),
        P(ROW + COL, None),
        P(),
        P(ROW, COL, None, None, None),
        P(ROW, COL, None),
        P(ROW, COL, None),
        P(ROW, COL),
    )

    def whole(grad_out, *rest):
        return jax.shard_map(
            functools.partial(body, grad_out.shape[0]),
            mesh=fine,
            in_specs=placed,
            out_specs=(P(ROW + COL, None), P()),
            check_vma=False,
        )(grad_out, *rest)

    return whole
```

```python
import functools

import jax
import jax.numpy as jnp
from jax import lax
from jax.experimental import pallas as pl
from jax.experimental.pallas import tpu as pltpu
from jax.sharding import Mesh
from jax.sharding import PartitionSpec as P

Z = ("za", "zb")
ROW = Z + ("core",)
COL = ("x", "y")


def tiles_kernel(count_ref, rows_ref, places_ref, values_ref, *refs):
    *pieces, features_ref, out_ref, share_ref, gathered, total, copied = refs
    row_tiles, tile, width = total.shape
    copies, first = [], 0
    for index, piece in enumerate(pieces):
        place = gathered.at[first : first + piece.shape[0]]
        copies.append(pltpu.make_async_copy(piece, place, copied.at[index]))
        first += piece.shape[0]
    for copy in copies:
        copy.start()
    total[...] = jnp.zeros_like(total)
    for copy in copies:
        copy.wait()

    def add(slot):
        row = rows_ref[slot]
        total[row] += jnp.dot(
            values_ref[slot], gathered[places_ref[slot]], preferred_element_type=jnp.float32
        )

    count = count_ref[0]
    fours = lax.shift_right_logical(count, 2)

    def four(index, carry):
        for offset in range(4):
            add(4 * index + offset)
        return carry

    def one(slot, carry):
        add(slot)
        return carry

    lax.fori_loop(0, fours, four, 0)
    lax.fori_loop(4 * fours, count, one, 0)

    step = 4
    grad = jnp.zeros((features_ref.shape[1], width), jnp.float32)
    for first in range(0, row_tiles, step):
        part = total[first : first + step].astype(jnp.bfloat16)
        out_ref[first : first + step] = part
        grad += lax.dot_general(
            features_ref[first * tile : (first + step) * tile],
            part.reshape(step * tile, width),
            (((0,), (0,)), ((), ())),
            preferred_element_type=jnp.float32,
        )
    share_ref[...] = grad.astype(jnp.bfloat16).reshape(share_ref.shape)


def sum_of(parts_ref):
    summed = parts_ref[0].astype(jnp.float32)
    for other in range(1, parts_ref.shape[0]):
        summed += parts_ref[other].astype(jnp.float32)
    return summed


def share_kernel(scale, shares_ref, share_ref):
    share_ref[...] = sum_of(shares_ref) * scale


def finish_kernel(parts_ref, weight_ref, input_ref):
    input_ref[...] = lax.dot_general(
        sum_of(parts_ref).astype(jnp.bfloat16),
        weight_ref[...],
        (((1,), (1,)), ((), ())),
        preferred_element_type=jnp.float32,
    ).astype(jnp.bfloat16)


def shifted(step):
    size = lax.axis_size(Z)
    return [(index, (index + step) % size) for index in range(size)]


def from_all(array, axes):
    size = lax.axis_size(axes)
    same = jnp.broadcast_to(array[None], (size, *array.shape))
    return lax.all_to_all(same, axes, 0, 0, tiled=True)


def gather_row(grad_out, beside):
    own, beside = lax.optimization_barrier((lax.all_gather(grad_out, "za"), beside))
    left, right = lax.ppermute(own, Z, shifted(1)), lax.ppermute(own, Z, shifted(-1))
    pieces = [own, left, right, lax.ppermute(right, Z, shifted(-1))]
    others = [lax.ppermute(piece, "core", [(0, 1), (1, 0)]) for piece in pieces]
    return *pieces, *others, beside


def place_of(block):
    high, residue, core = block >> 3, (block >> 1) & 3, block & 1
    away = (residue - lax.axis_index("zb")) & 3
    group = jnp.where(away == 3, 1, jnp.where(away == 0, 0, away + 1))
    return (core ^ lax.axis_index("core")) * 32 + group * 8 + high


def body(nodes, grad_out, features, weight, tile_values, tile_rows, tile_cols, tile_count):
    tile = tile_values.shape[-1]
    width = grad_out.shape[1]
    cols = lax.axis_size(COL)
    share = width // cols
    own_features = from_all(features, COL).reshape(-1, width)
    *pieces, own_features = gather_row(grad_out, own_features)
    smem, vmem = pl.BlockSpec(memory_space=pltpu.SMEM), pl.BlockSpec(memory_space=pltpu.VMEM)
    anywhere = pl.BlockSpec(memory_space=pl.ANY)
    parts, shares = pl.pallas_call(
        tiles_kernel,
        out_shape=(
            jax.ShapeDtypeStruct((cols, tile, width), jnp.bfloat16),
            jax.ShapeDtypeStruct((cols, share, width), jnp.bfloat16),
        ),
        in_specs=[smem] * 3 + [vmem] + [anywhere] * len(pieces) + [vmem],
        out_specs=(vmem, vmem),
        scratch_shapes=[
            pltpu.VMEM((lax.axis_size(ROW), tile, width), jnp.bfloat16),
            pltpu.VMEM((cols, tile, width), jnp.float32),
            pltpu.SemaphoreType.DMA((len(pieces),)),
        ],
        compiler_params=pltpu.CompilerParams(vmem_limit_bytes=24 * 2**20),
    )(
        tile_count[0],
        tile_rows[0, 0],
        place_of(tile_cols[0, 0]),
        tile_values[0, 0],
        *pieces,
        own_features,
    )
    shares = lax.all_to_all(shares, COL, 0, 0, tiled=True)
    grad_share = pl.pallas_call(
        functools.partial(share_kernel, nodes**-0.5),
        out_shape=jax.ShapeDtypeStruct((share, width), jnp.float32),
        in_specs=[vmem],
        out_specs=vmem,
        compiler_params=pltpu.CompilerParams(vmem_limit_bytes=4 * 2**20),
    )(shares)
    grad_share = jnp.sum(from_all(grad_share, ("zb", "core")), axis=0)
    grad_share, parts = lax.optimization_barrier((grad_share, parts))
    parts = lax.all_to_all(parts, COL, 0, 0, tiled=True)
    grad_share, parts = lax.optimization_barrier((lax.all_gather(grad_share, "za"), parts))
    grad_share = jnp.sum(grad_share, axis=0).astype(jnp.bfloat16)
    weight_grad = from_all(grad_share, COL).reshape(width, width).astype(jnp.float32)
    input_grad = pl.pallas_call(
        finish_kernel,
        out_shape=jax.ShapeDtypeStruct((tile, width), jnp.bfloat16),
        in_specs=[vmem] * 2,
        out_specs=vmem,
        compiler_params=pltpu.CompilerParams(vmem_limit_bytes=8 * 2**20),
    )(parts, weight)
    return input_grad, weight_grad


def solution(mesh):
    fine = Mesh(mesh.devices.reshape(8, 4, 2, 4, 4), ROW + COL)
    placed = (
        P(COL + ROW, None),
        P(ROW + COL, None),
        P(),
        P(ROW, COL, None, None, None),
        P(ROW, COL, None),
        P(ROW, COL, None),
        P(ROW, COL),
    )

    def whole(grad_out, *rest):
        return jax.shard_map(
            functools.partial(body, grad_out.shape[0]),
            mesh=fine,
            in_specs=placed,
            out_specs=(P(ROW + COL, None), P()),
            check_vma=False,
        )(grad_out, *rest)

    return whole
```

```python
import functools

import jax
import jax.numpy as jnp
from jax import lax
from jax.experimental import pallas as pl
from jax.experimental.pallas import tpu as pltpu
from jax.sharding import Mesh
from jax.sharding import PartitionSpec as P

Z = ("za", "zb")
ROW = Z + ("core",)
COL = ("x", "y")


def tiles_kernel(count_ref, rows_ref, places_ref, values_ref, *refs):
    *pieces, features_ref, out_ref, share_ref, gathered, total, copied = refs
    row_tiles, tile, width = total.shape
    copies, first = [], 0
    for index, piece in enumerate(pieces):
        place = gathered.at[first : first + piece.shape[0]]
        copies.append(pltpu.make_async_copy(piece, place, copied.at[index]))
        first += piece.shape[0]
    for copy in copies:
        copy.start()
    total[...] = jnp.zeros_like(total)
    for copy in copies:
        copy.wait()

    def add(slot):
        row = rows_ref[slot]
        total[row] += jnp.dot(
            values_ref[slot], gathered[places_ref[slot]], preferred_element_type=jnp.float32
        )

    count = count_ref[0]
    fours = lax.shift_right_logical(count, 2)

    def four(index, carry):
        for offset in range(4):
            add(4 * index + offset)
        return carry

    def one(slot, carry):
        add(slot)
        return carry

    lax.fori_loop(0, fours, four, 0)
    lax.fori_loop(4 * fours, count, one, 0)

    step = 4
    grad = jnp.zeros((features_ref.shape[1], width), jnp.float32)
    for first in range(0, row_tiles, step):
        part = total[first : first + step].astype(jnp.bfloat16)
        out_ref[first : first + step] = part
        grad += lax.dot_general(
            features_ref[first * tile : (first + step) * tile],
            part.reshape(step * tile, width),
            (((0,), (0,)), ((), ())),
            preferred_element_type=jnp.float32,
        )
    share_ref[...] = grad.astype(jnp.bfloat16).reshape(share_ref.shape)


def sum_of(parts_ref):
    summed = parts_ref[0].astype(jnp.float32)
    for other in range(1, parts_ref.shape[0]):
        summed += parts_ref[other].astype(jnp.float32)
    return summed


def sum_kernel(scale, shares_ref, share_ref):
    share_ref[...] = sum_of(shares_ref) * scale


def sum_and_copy_kernel(scale, shares_ref, copies_ref):
    summed = (sum_of(shares_ref) * scale).astype(copies_ref.dtype)
    copies_ref[...] = jnp.broadcast_to(summed[None], copies_ref.shape)


def finish_kernel(parts_ref, weight_ref, input_ref):
    input_ref[...] = lax.dot_general(
        sum_of(parts_ref).astype(jnp.bfloat16),
        weight_ref[...],
        (((1,), (1,)), ((), ())),
        preferred_element_type=jnp.float32,
    ).astype(jnp.bfloat16)


def shifted(step):
    size = lax.axis_size(Z)
    return [(index, (index + step) % size) for index in range(size)]


def from_all(array, axes):
    size = lax.axis_size(axes)
    same = jnp.broadcast_to(array[None], (size, *array.shape))
    return lax.all_to_all(same, axes, 0, 0, tiled=True)


def gather_row(grad_out, later):
    own, later = lax.optimization_barrier((lax.all_gather(grad_out, "za"), later))
    swap = [(0, 1), (1, 0)]
    left, right = lax.ppermute(own, Z, shifted(1)), lax.ppermute(own, Z, shifted(-1))
    onward, swapped = lax.optimization_barrier((right, lax.ppermute(own, "core", swap)))
    opposite = lax.ppermute(onward, Z, shifted(-1))
    others = [lax.ppermute(piece, "core", swap) for piece in (left, right, opposite)]
    return own, left, right, opposite, swapped, *others, later


def place_of(block):
    high, residue, core = block >> 3, (block >> 1) & 3, block & 1
    away = (residue - lax.axis_index("zb")) & 3
    group = jnp.where(away == 3, 1, jnp.where(away == 0, 0, away + 1))
    return (core ^ lax.axis_index("core")) * 32 + group * 8 + high


def body(nodes, grad_out, features, weight, tile_values, tile_rows, tile_cols, tile_count):
    tile = tile_values.shape[-1]
    width = grad_out.shape[1]
    cols = lax.axis_size(COL)
    share = width // cols
    *pieces, features = gather_row(grad_out, features)
    own_features = from_all(features, COL).reshape(-1, width)
    smem, vmem = pl.BlockSpec(memory_space=pltpu.SMEM), pl.BlockSpec(memory_space=pltpu.VMEM)
    anywhere = pl.BlockSpec(memory_space=pl.ANY)
    parts, shares = pl.pallas_call(
        tiles_kernel,
        out_shape=(
            jax.ShapeDtypeStruct((cols, tile, width), jnp.bfloat16),
            jax.ShapeDtypeStruct((cols, share, width), jnp.bfloat16),
        ),
        in_specs=[smem] * 3 + [vmem] + [anywhere] * len(pieces) + [vmem],
        out_specs=(vmem, vmem),
        scratch_shapes=[
            pltpu.VMEM((lax.axis_size(ROW), tile, width), jnp.bfloat16),
            pltpu.VMEM((cols, tile, width), jnp.float32),
            pltpu.SemaphoreType.DMA((len(pieces),)),
        ],
        compiler_params=pltpu.CompilerParams(vmem_limit_bytes=24 * 2**20),
    )(
        tile_count[0],
        tile_rows[0, 0],
        place_of(tile_cols[0, 0]),
        tile_values[0, 0],
        *pieces,
        own_features,
    )
    shares = lax.all_to_all(shares, COL, 0, 0, tiled=True)

    def summed(kernel, shape, dtype, array, scale=1.0):
        return pl.pallas_call(
            functools.partial(kernel, scale),
            out_shape=jax.ShapeDtypeStruct(shape, dtype),
            in_specs=[vmem],
            out_specs=vmem,
            compiler_params=pltpu.CompilerParams(vmem_limit_bytes=4 * 2**20),
        )(array)

    near, far = ("zb", "core"), "za"
    shares = summed(sum_and_copy_kernel, (lax.axis_size(near), share, width), jnp.float32, shares, nodes**-0.5)
    grad_share = summed(sum_kernel, (share, width), jnp.float32, lax.all_to_all(shares, near, 0, 0, tiled=True))
    grad_share, parts = lax.optimization_barrier((grad_share, parts))
    parts = lax.all_to_all(parts, COL, 0, 0, tiled=True)
    shares, parts = lax.optimization_barrier((lax.all_gather(grad_share, far), parts))
    shares = summed(sum_and_copy_kernel, (cols, share, width), jnp.bfloat16, shares)
    weight_grad = lax.all_to_all(shares, COL, 0, 0, tiled=True).reshape(width, width).astype(jnp.float32)
    input_grad = pl.pallas_call(
        finish_kernel,
        out_shape=jax.ShapeDtypeStruct((tile, width), jnp.bfloat16),
        in_specs=[vmem] * 2,
        out_specs=vmem,
        compiler_params=pltpu.CompilerParams(vmem_limit_bytes=8 * 2**20),
    )(parts, weight)
    return input_grad, weight_grad


def solution(mesh):
    fine = Mesh(mesh.devices.reshape(8, 4, 2, 4, 4), ROW + COL)
    placed = (
        P(COL + ROW, None),
        P(ROW + COL, None),
        P(),
        P(ROW, COL, None, None, None),
        P(ROW, COL, None),
        P(ROW, COL, None),
        P(ROW, COL),
    )

    def whole(grad_out, *rest):
        return jax.shard_map(
            functools.partial(body, grad_out.shape[0]),
            mesh=fine,
            in_specs=placed,
            out_specs=(P(ROW + COL, None), P()),
            check_vma=False,
        )(grad_out, *rest)

    return whole
```

```python
import functools

import jax
import jax.numpy as jnp
from jax import lax
from jax.experimental import pallas as pl
from jax.experimental.pallas import tpu as pltpu
from jax.sharding import Mesh
from jax.sharding import PartitionSpec as P

Z = ("za", "zb")
ROW = Z + ("core",)
COL = ("x", "y")


def tiles_kernel(count_ref, rows_ref, places_ref, values_ref, *refs):
    *pieces, features_ref, out_ref, share_ref, gathered, total, copied = refs
    row_tiles, tile, width = total.shape
    copies, first = [], 0
    for index, piece in enumerate(pieces):
        place = gathered.at[first : first + piece.shape[0]]
        copies.append(pltpu.make_async_copy(piece, place, copied.at[index]))
        first += piece.shape[0]
    for copy in copies:
        copy.start()
    total[...] = jnp.zeros_like(total)
    for copy in copies:
        copy.wait()

    def add(slot):
        row = rows_ref[slot]
        total[row] += jnp.dot(
            values_ref[slot], gathered[places_ref[slot]], preferred_element_type=jnp.float32
        )

    count = count_ref[0]
    fours = lax.shift_right_logical(count, 2)

    def four(index, carry):
        for offset in range(4):
            add(4 * index + offset)
        return carry

    def one(slot, carry):
        add(slot)
        return carry

    lax.fori_loop(0, fours, four, 0)
    lax.fori_loop(4 * fours, count, one, 0)

    step = 4
    grad = jnp.zeros((features_ref.shape[1], width), jnp.float32)
    for first in range(0, row_tiles, step):
        part = total[first : first + step].astype(jnp.bfloat16)
        out_ref[first : first + step] = part
        grad += lax.dot_general(
            features_ref[first * tile : (first + step) * tile],
            part.reshape(step * tile, width),
            (((0,), (0,)), ((), ())),
            preferred_element_type=jnp.float32,
        )
    share_ref[...] = grad.astype(jnp.bfloat16).reshape(share_ref.shape)


def sum_of(parts_ref):
    summed = parts_ref[0].astype(jnp.float32)
    for other in range(1, parts_ref.shape[0]):
        summed += parts_ref[other].astype(jnp.float32)
    return summed


def sum_kernel(scale, shares_ref, share_ref):
    share_ref[...] = sum_of(shares_ref) * scale


def sum_and_copy_kernel(scale, shares_ref, copies_ref):
    summed = (sum_of(shares_ref) * scale).astype(copies_ref.dtype)
    copies_ref[...] = jnp.broadcast_to(summed[None], copies_ref.shape)


def finish_kernel(parts_ref, weight_ref, input_ref):
    input_ref[...] = lax.dot_general(
        sum_of(parts_ref).astype(jnp.bfloat16),
        weight_ref[...],
        (((1,), (1,)), ((), ())),
        preferred_element_type=jnp.float32,
    ).astype(jnp.bfloat16)


def shifted(step):
    size = lax.axis_size(Z)
    return [(index, (index + step) % size) for index in range(size)]


def from_all(array, axes):
    size = lax.axis_size(axes)
    same = jnp.broadcast_to(array[None], (size, *array.shape))
    return lax.all_to_all(same, axes, 0, 0, tiled=True)


def gather(grad_out, features):
    own, features = lax.optimization_barrier((lax.all_gather(grad_out, "za"), features))
    swap = [(0, 1), (1, 0)]
    left, right = lax.ppermute(own, Z, shifted(1)), lax.ppermute(own, Z, shifted(-1))
    features = from_all(features, COL)
    opposite = lax.ppermute(right, Z, shifted(-1))
    left_ready, features = lax.optimization_barrier((left, features))
    others = [lax.ppermute(piece, "core", swap) for piece in (own, left_ready, right, opposite)]
    return own, left, right, opposite, *others, features.reshape(-1, features.shape[-1])


def place_of(block):
    high, residue, core = block >> 3, (block >> 1) & 3, block & 1
    away = (residue - lax.axis_index("zb")) & 3
    group = jnp.where(away == 3, 1, jnp.where(away == 0, 0, away + 1))
    return (core ^ lax.axis_index("core")) * 32 + group * 8 + high


def body(nodes, grad_out, features, weight, tile_values, tile_rows, tile_cols, tile_count):
    tile = tile_values.shape[-1]
    width = grad_out.shape[1]
    cols = lax.axis_size(COL)
    share = width // cols
    *pieces, own_features = gather(grad_out, features)
    smem, vmem = pl.BlockSpec(memory_space=pltpu.SMEM), pl.BlockSpec(memory_space=pltpu.VMEM)
    anywhere = pl.BlockSpec(memory_space=pl.ANY)
    parts, shares = pl.pallas_call(
        tiles_kernel,
        out_shape=(
            jax.ShapeDtypeStruct((cols, tile, width), jnp.bfloat16),
            jax.ShapeDtypeStruct((cols, share, width), jnp.bfloat16),
        ),
        in_specs=[smem] * 3 + [vmem] + [anywhere] * len(pieces) + [vmem],
        out_specs=(vmem, vmem),
        scratch_shapes=[
            pltpu.VMEM((lax.axis_size(ROW), tile, width), jnp.bfloat16),
            pltpu.VMEM((cols, tile, width), jnp.float32),
            pltpu.SemaphoreType.DMA((len(pieces),)),
        ],
        compiler_params=pltpu.CompilerParams(vmem_limit_bytes=24 * 2**20),
    )(
        tile_count[0],
        tile_rows[0, 0],
        place_of(tile_cols[0, 0]),
        tile_values[0, 0],
        *pieces,
        own_features,
    )
    shares = lax.all_to_all(shares, COL, 0, 0, tiled=True)

    def summed(kernel, shape, dtype, array, scale=1.0):
        return pl.pallas_call(
            functools.partial(kernel, scale),
            out_shape=jax.ShapeDtypeStruct(shape, dtype),
            in_specs=[vmem],
            out_specs=vmem,
            compiler_params=pltpu.CompilerParams(vmem_limit_bytes=4 * 2**20),
        )(array)

    near, far = ("zb", "core"), "za"
    shares = summed(sum_and_copy_kernel, (lax.axis_size(near), share, width), jnp.float32, shares, nodes**-0.5)
    grad_share = summed(sum_kernel, (share, width), jnp.float32, lax.all_to_all(shares, near, 0, 0, tiled=True))
    grad_share, parts = lax.optimization_barrier((grad_share, parts))
    parts = lax.all_to_all(parts, COL, 0, 0, tiled=True)
    shares, parts = lax.optimization_barrier((lax.all_gather(grad_share, far), parts))
    shares = summed(sum_and_copy_kernel, (cols, share, width), jnp.bfloat16, shares)
    weight_grad = lax.all_to_all(shares, COL, 0, 0, tiled=True).reshape(width, width).astype(jnp.float32)
    input_grad = pl.pallas_call(
        finish_kernel,
        out_shape=jax.ShapeDtypeStruct((tile, width), jnp.bfloat16),
        in_specs=[vmem] * 2,
        out_specs=vmem,
        compiler_params=pltpu.CompilerParams(vmem_limit_bytes=8 * 2**20),
    )(parts, weight)
    return input_grad, weight_grad


def solution(mesh):
    fine = Mesh(mesh.devices.reshape(8, 4, 2, 4, 4), ROW + COL)
    placed = (
        P(COL + ROW, None),
        P(ROW + COL, None),
        P(),
        P(ROW, COL, None, None, None),
        P(ROW, COL, None),
        P(ROW, COL, None),
        P(ROW, COL),
    )

    def whole(grad_out, *rest):
        return jax.shard_map(
            functools.partial(body, grad_out.shape[0]),
            mesh=fine,
            in_specs=placed,
            out_specs=(P(ROW + COL, None), P()),
            check_vma=False,
        )(grad_out, *rest)

    return whole
```

```python
import functools

import jax
import jax.numpy as jnp
from jax import lax
from jax.experimental import pallas as pl
from jax.experimental.pallas import tpu as pltpu
from jax.sharding import Mesh
from jax.sharding import PartitionSpec as P

Z = ("za", "zb")
ROW = Z + ("core",)
COL = ("x", "y")
SHARE = ("core", "y")


def tiles_kernel(count_ref, rows_ref, places_ref, values_ref, *refs):
    *pieces, features_ref, out_ref, share_ref, gathered, total, copied = refs
    row_tiles, tile, width = total.shape
    copies, first = [], 0
    for index, piece in enumerate(pieces):
        place = gathered.at[first : first + piece.shape[0]]
        copies.append(pltpu.make_async_copy(piece, place, copied.at[index]))
        first += piece.shape[0]
    for copy in copies:
        copy.start()
    total[...] = jnp.zeros_like(total)
    for copy in copies:
        copy.wait()

    def add(slot):
        row = rows_ref[slot]
        total[row] += jnp.dot(
            values_ref[slot], gathered[places_ref[slot]], preferred_element_type=jnp.float32
        )

    count = count_ref[0]
    fours = lax.shift_right_logical(count, 2)

    def four(index, carry):
        for offset in range(4):
            add(4 * index + offset)
        return carry

    def one(slot, carry):
        add(slot)
        return carry

    lax.fori_loop(0, fours, four, 0)
    lax.fori_loop(4 * fours, count, one, 0)

    step = 4
    grad = jnp.zeros((features_ref.shape[1], width), jnp.float32)
    for first in range(0, row_tiles, step):
        part = total[first : first + step].astype(jnp.bfloat16)
        out_ref[first : first + step] = part
        grad += lax.dot_general(
            features_ref[first * tile : (first + step) * tile],
            part.reshape(step * tile, width),
            (((0,), (0,)), ((), ())),
            preferred_element_type=jnp.float32,
        )
    share_ref[...] = grad.astype(jnp.bfloat16).reshape(share_ref.shape)


def sum_of(parts_ref):
    summed = parts_ref[0].astype(jnp.float32)
    for other in range(1, parts_ref.shape[0]):
        summed += parts_ref[other].astype(jnp.float32)
    return summed


def sum_kernel(scale, shares_ref, share_ref):
    share_ref[...] = sum_of(shares_ref) * scale


def sum_and_copy_kernel(scale, shares_ref, copies_ref):
    summed = (sum_of(shares_ref) * scale).astype(copies_ref.dtype)
    copies_ref[...] = jnp.broadcast_to(summed[None], copies_ref.shape)


def finish_kernel(parts_ref, weight_ref, input_ref):
    input_ref[...] = lax.dot_general(
        sum_of(parts_ref).astype(jnp.bfloat16),
        weight_ref[...],
        (((1,), (1,)), ((), ())),
        preferred_element_type=jnp.float32,
    ).astype(jnp.bfloat16)


def shifted(step):
    size = lax.axis_size(Z)
    return [(index, (index + step) % size) for index in range(size)]


def from_all(array, axes):
    size = lax.axis_size(axes)
    same = jnp.broadcast_to(array[None], (size, *array.shape))
    return lax.all_to_all(same, axes, 0, 0, tiled=True)


def gather(grad_out, features):
    own, features = lax.optimization_barrier((lax.all_gather(grad_out, "za"), features))
    swap = [(0, 1), (1, 0)]
    left, right = lax.ppermute(own, Z, shifted(1)), lax.ppermute(own, Z, shifted(-1))
    features = from_all(features, COL)
    opposite = lax.ppermute(right, Z, shifted(-1))
    left_ready, features = lax.optimization_barrier((left, features))
    others = [lax.ppermute(piece, "core", swap) for piece in (own, left_ready, right, opposite)]
    return own, left, right, opposite, *others, features.reshape(-1, features.shape[-1])


def place_of(block):
    high, residue, core = block >> 3, (block >> 1) & 3, block & 1
    away = (residue - lax.axis_index("zb")) & 3
    group = jnp.where(away == 3, 1, jnp.where(away == 0, 0, away + 1))
    return (core ^ lax.axis_index("core")) * 32 + group * 8 + high


def body(nodes, grad_out, features, weight, tile_values, tile_rows, tile_cols, tile_count):
    tile = tile_values.shape[-1]
    width = grad_out.shape[1]
    cols = lax.axis_size(COL)
    sharers = lax.axis_size(SHARE)
    share = width // sharers
    *pieces, own_features = gather(grad_out, features)
    smem, vmem = pl.BlockSpec(memory_space=pltpu.SMEM), pl.BlockSpec(memory_space=pltpu.VMEM)
    anywhere = pl.BlockSpec(memory_space=pl.ANY)
    parts, shares = pl.pallas_call(
        tiles_kernel,
        out_shape=(
            jax.ShapeDtypeStruct((cols, tile, width), jnp.bfloat16),
            jax.ShapeDtypeStruct((sharers, share, width), jnp.bfloat16),
        ),
        in_specs=[smem] * 3 + [vmem] + [anywhere] * len(pieces) + [vmem],
        out_specs=(vmem, vmem),
        scratch_shapes=[
            pltpu.VMEM((lax.axis_size(ROW), tile, width), jnp.bfloat16),
            pltpu.VMEM((cols, tile, width), jnp.float32),
            pltpu.SemaphoreType.DMA((len(pieces),)),
        ],
        compiler_params=pltpu.CompilerParams(vmem_limit_bytes=24 * 2**20),
    )(
        tile_count[0],
        tile_rows[0, 0],
        place_of(tile_cols[0, 0]),
        tile_values[0, 0],
        *pieces,
        own_features,
    )
    shares = lax.all_to_all(shares, SHARE, 0, 0, tiled=True)

    def summed(kernel, shape, dtype, array, scale=1.0):
        return pl.pallas_call(
            functools.partial(kernel, scale),
            out_shape=jax.ShapeDtypeStruct(shape, dtype),
            in_specs=[vmem],
            out_specs=vmem,
            compiler_params=pltpu.CompilerParams(vmem_limit_bytes=4 * 2**20),
        )(array)

    scale = nodes**-0.5
    for axis in ("x", "zb"):
        copies = (lax.axis_size(axis), share, width)
        shares = lax.all_to_all(summed(sum_and_copy_kernel, copies, jnp.float32, shares, scale), axis, 0, 0, tiled=True)
        scale = 1.0
    grad_share = summed(sum_kernel, (share, width), jnp.float32, shares)
    grad_share, parts = lax.optimization_barrier((grad_share, parts))
    parts = lax.all_to_all(parts, COL, 0, 0, tiled=True)
    shares, parts = lax.optimization_barrier((lax.all_gather(grad_share, "za"), parts))
    shares = summed(sum_and_copy_kernel, (sharers, share, width), jnp.bfloat16, shares)
    weight_grad = lax.all_to_all(shares, SHARE, 0, 0, tiled=True).reshape(width, width).astype(jnp.float32)
    input_grad = pl.pallas_call(
        finish_kernel,
        out_shape=jax.ShapeDtypeStruct((tile, width), jnp.bfloat16),
        in_specs=[vmem] * 2,
        out_specs=vmem,
        compiler_params=pltpu.CompilerParams(vmem_limit_bytes=8 * 2**20),
    )(parts, weight)
    return input_grad, weight_grad


def solution(mesh):
    fine = Mesh(mesh.devices.reshape(8, 4, 2, 4, 4), ROW + COL)
    placed = (
        P(COL + ROW, None),
        P(ROW + COL, None),
        P(),
        P(ROW, COL, None, None, None),
        P(ROW, COL, None),
        P(ROW, COL, None),
        P(ROW, COL),
    )

    def whole(grad_out, *rest):
        return jax.shard_map(
            functools.partial(body, grad_out.shape[0]),
            mesh=fine,
            in_specs=placed,
            out_specs=(P(ROW + COL, None), P()),
            check_vma=False,
        )(grad_out, *rest)

    return whole
```

```python
import functools

import jax
import jax.numpy as jnp
from jax import lax
from jax.experimental import pallas as pl
from jax.experimental.pallas import tpu as pltpu
from jax.sharding import Mesh
from jax.sharding import PartitionSpec as P

Z = ("za", "zb")
ROW = Z + ("core",)
COL = ("x", "y")


def tiles_kernel(count_ref, rows_ref, places_ref, values_ref, *refs):
    *pieces, features_ref, out_ref, share_ref, gathered, total, copied = refs
    row_tiles, tile, width = total.shape
    copies, first = [], 0
    for index, piece in enumerate(pieces):
        place = gathered.at[first : first + piece.shape[0]]
        copies.append(pltpu.make_async_copy(piece, place, copied.at[index]))
        first += piece.shape[0]
    for copy in copies:
        copy.start()
    total[...] = jnp.zeros_like(total)
    for copy in copies:
        copy.wait()

    def add(slot):
        row = rows_ref[slot]
        total[row] += jnp.dot(
            values_ref[slot], gathered[places_ref[slot]], preferred_element_type=jnp.float32
        )

    count, done = count_ref[0], 0
    for bits in (4, 2, 0):
        groups = lax.shift_right_logical(count - done, bits)

        def group(index, first, bits=bits):
            for offset in range(2**bits):
                add(first + offset)
            return first + 2**bits

        done = lax.fori_loop(0, groups, group, done)

    step = 4
    grad = jnp.zeros((features_ref.shape[1], width), jnp.float32)
    for first in range(0, row_tiles, step):
        part = total[first : first + step].astype(jnp.bfloat16)
        out_ref[first : first + step] = part
        grad += lax.dot_general(
            features_ref[first * tile : (first + step) * tile],
            part.reshape(step * tile, width),
            (((0,), (0,)), ((), ())),
            preferred_element_type=jnp.float32,
        )
    share_ref[...] = grad.astype(jnp.bfloat16).reshape(share_ref.shape)


def sum_of(parts_ref):
    summed = parts_ref[0].astype(jnp.float32)
    for other in range(1, parts_ref.shape[0]):
        summed += parts_ref[other].astype(jnp.float32)
    return summed


def sum_kernel(scale, shares_ref, share_ref):
    share_ref[...] = sum_of(shares_ref) * scale


def sum_and_copy_kernel(scale, shares_ref, copies_ref):
    summed = (sum_of(shares_ref) * scale).astype(copies_ref.dtype)
    copies_ref[...] = jnp.broadcast_to(summed[None], copies_ref.shape)


def finish_kernel(parts_ref, weight_ref, input_ref):
    input_ref[...] = lax.dot_general(
        sum_of(parts_ref).astype(jnp.bfloat16),
        weight_ref[...],
        (((1,), (1,)), ((), ())),
        preferred_element_type=jnp.float32,
    ).astype(jnp.bfloat16)


def shifted(step):
    size = lax.axis_size(Z)
    return [(index, (index + step) % size) for index in range(size)]


def from_all(array, axes):
    size = lax.axis_size(axes)
    same = jnp.broadcast_to(array[None], (size, *array.shape))
    return lax.all_to_all(same, axes, 0, 0, tiled=True)


def gather(grad_out, features):
    own, features = lax.optimization_barrier((lax.all_gather(grad_out, "za"), features))
    swap = [(0, 1), (1, 0)]
    left, right = lax.ppermute(own, Z, shifted(1)), lax.ppermute(own, Z, shifted(-1))
    features = from_all(features, COL)
    opposite = lax.ppermute(right, Z, shifted(-1))
    left_ready, features = lax.optimization_barrier((left, features))
    others = [lax.ppermute(piece, "core", swap) for piece in (own, left_ready, right, opposite)]
    return own, left, right, opposite, *others, features.reshape(-1, features.shape[-1])


def place_of(block):
    high, residue, core = block >> 3, (block >> 1) & 3, block & 1
    away = (residue - lax.axis_index("zb")) & 3
    group = jnp.where(away == 3, 1, jnp.where(away == 0, 0, away + 1))
    return (core ^ lax.axis_index("core")) * 32 + group * 8 + high


def body(nodes, grad_out, features, weight, tile_values, tile_rows, tile_cols, tile_count):
    tile = tile_values.shape[-1]
    width = grad_out.shape[1]
    cols = lax.axis_size(COL)
    share = width // cols
    *pieces, own_features = gather(grad_out, features)
    smem, vmem = pl.BlockSpec(memory_space=pltpu.SMEM), pl.BlockSpec(memory_space=pltpu.VMEM)
    anywhere = pl.BlockSpec(memory_space=pl.ANY)
    parts, shares = pl.pallas_call(
        tiles_kernel,
        out_shape=(
            jax.ShapeDtypeStruct((cols, tile, width), jnp.bfloat16),
            jax.ShapeDtypeStruct((cols, share, width), jnp.bfloat16),
        ),
        in_specs=[smem] * 3 + [vmem] + [anywhere] * len(pieces) + [vmem],
        out_specs=(vmem, vmem),
        scratch_shapes=[
            pltpu.VMEM((lax.axis_size(ROW), tile, width), jnp.bfloat16),
            pltpu.VMEM((cols, tile, width), jnp.float32),
            pltpu.SemaphoreType.DMA((len(pieces),)),
        ],
        compiler_params=pltpu.CompilerParams(vmem_limit_bytes=24 * 2**20),
    )(
        tile_count[0],
        tile_rows[0, 0],
        place_of(tile_cols[0, 0]),
        tile_values[0, 0],
        *pieces,
        own_features,
    )
    shares = lax.all_to_all(shares, COL, 0, 0, tiled=True)

    def summed(kernel, shape, dtype, array, scale=1.0):
        return pl.pallas_call(
            functools.partial(kernel, scale),
            out_shape=jax.ShapeDtypeStruct(shape, dtype),
            in_specs=[vmem],
            out_specs=vmem,
            compiler_params=pltpu.CompilerParams(vmem_limit_bytes=4 * 2**20),
        )(array)

    near, far = ("zb", "core"), "za"
    shares = summed(sum_and_copy_kernel, (lax.axis_size(near), share, width), jnp.float32, shares, nodes**-0.5)
    grad_share = summed(sum_kernel, (share, width), jnp.float32, lax.all_to_all(shares, near, 0, 0, tiled=True))
    grad_share, parts = lax.optimization_barrier((grad_share, parts))
    parts = lax.all_to_all(parts, COL, 0, 0, tiled=True)
    shares, parts = lax.optimization_barrier((lax.all_gather(grad_share, far), parts))
    shares = summed(sum_and_copy_kernel, (cols, share, width), jnp.bfloat16, shares)
    weight_grad = lax.all_to_all(shares, COL, 0, 0, tiled=True).reshape(width, width).astype(jnp.float32)
    input_grad = pl.pallas_call(
        finish_kernel,
        out_shape=jax.ShapeDtypeStruct((tile, width), jnp.bfloat16),
        in_specs=[vmem] * 2,
        out_specs=vmem,
        compiler_params=pltpu.CompilerParams(vmem_limit_bytes=8 * 2**20),
    )(parts, weight)
    return input_grad, weight_grad


def solution(mesh):
    fine = Mesh(mesh.devices.reshape(8, 4, 2, 4, 4), ROW + COL)
    placed = (
        P(COL + ROW, None),
        P(ROW + COL, None),
        P(),
        P(ROW, COL, None, None, None),
        P(ROW, COL, None),
        P(ROW, COL, None),
        P(ROW, COL),
    )

    def whole(grad_out, *rest):
        return jax.shard_map(
            functools.partial(body, grad_out.shape[0]),
            mesh=fine,
            in_specs=placed,
            out_specs=(P(ROW + COL, None), P()),
            check_vma=False,
        )(grad_out, *rest)

    return whole
```

```python
import functools

import jax
import jax.numpy as jnp
from jax import lax
from jax.experimental import pallas as pl
from jax.experimental.pallas import tpu as pltpu
from jax.sharding import Mesh
from jax.sharding import PartitionSpec as P

Z = ("za", "zb")
ROW = Z + ("core",)
COL = ("x", "y")


def tiles_kernel(count_ref, rows_ref, places_ref, values_ref, *refs):
    *pieces, features_ref, out_ref, share_ref, gathered, total, copied = refs
    row_tiles, tile, width = total.shape
    copies, first = [], 0
    for index, piece in enumerate(pieces):
        place = gathered.at[first : first + piece.shape[0]]
        copies.append(pltpu.make_async_copy(piece, place, copied.at[index]))
        first += piece.shape[0]
    for copy in copies:
        copy.start()
    total[...] = jnp.zeros_like(total)
    for copy in copies:
        copy.wait()

    def add(slot):
        row = rows_ref[slot]
        total[row] += jnp.dot(
            values_ref[slot], gathered[places_ref[slot]], preferred_element_type=jnp.float32
        )

    count, done = count_ref[0], 0
    for bits in (4, 2, 0):
        groups = lax.shift_right_logical(count - done, bits)

        def group(index, first, bits=bits):
            for offset in range(2**bits):
                add(first + offset)
            return first + 2**bits

        done = lax.fori_loop(0, groups, group, done)

    step = 4
    grad = jnp.zeros((features_ref.shape[1], width), jnp.float32)
    for first in range(0, row_tiles, step):
        part = total[first : first + step].astype(jnp.bfloat16)
        out_ref[first : first + step] = part
        grad += lax.dot_general(
            features_ref[first * tile : (first + step) * tile],
            part.reshape(step * tile, width),
            (((0,), (0,)), ((), ())),
            preferred_element_type=jnp.float32,
        )
    share_ref[...] = grad.astype(jnp.bfloat16).reshape(share_ref.shape)


def sum_of(parts_ref):
    summed = parts_ref[0].astype(jnp.float32)
    for other in range(1, parts_ref.shape[0]):
        summed += parts_ref[other].astype(jnp.float32)
    return summed


def sum_kernel(scale, shares_ref, share_ref):
    share_ref[...] = sum_of(shares_ref) * scale


def sum_and_copy_kernel(scale, shares_ref, copies_ref):
    summed = (sum_of(shares_ref) * scale).astype(copies_ref.dtype)
    copies_ref[...] = jnp.broadcast_to(summed[None], copies_ref.shape)


def finish_kernel(parts_ref, weight_ref, input_ref):
    input_ref[...] = lax.dot_general(
        sum_of(parts_ref).astype(jnp.bfloat16),
        weight_ref[...],
        (((1,), (1,)), ((), ())),
        preferred_element_type=jnp.float32,
    ).astype(jnp.bfloat16)


def shifted(step):
    size = lax.axis_size(Z)
    return [(index, (index + step) % size) for index in range(size)]


def from_all(array, axes):
    size = lax.axis_size(axes)
    same = jnp.broadcast_to(array[None], (size, *array.shape))
    return lax.all_to_all(same, axes, 0, 0, tiled=True)


def gather(grad_out, features):
    own, features = lax.optimization_barrier((lax.all_gather(grad_out, "za"), features))
    swap = [(0, 1), (1, 0)]
    left, right = lax.ppermute(own, Z, shifted(1)), lax.ppermute(own, Z, shifted(-1))
    features = from_all(features, COL)
    opposite = lax.ppermute(right, Z, shifted(-1))
    left_ready, features = lax.optimization_barrier((left, features))
    others = [lax.ppermute(piece, "core", swap) for piece in (own, left_ready, right, opposite)]
    return own, left, right, opposite, *others, features.reshape(-1, features.shape[-1])


def place_of(block):
    high, residue, core = block >> 3, (block >> 1) & 3, block & 1
    away = (residue - lax.axis_index("zb")) & 3
    group = jnp.where(away == 3, 1, jnp.where(away == 0, 0, away + 1))
    return (core ^ lax.axis_index("core")) * 32 + group * 8 + high


def body(nodes, grad_out, features, weight, tile_values, tile_rows, tile_cols, tile_count):
    tile = tile_values.shape[-1]
    width = grad_out.shape[1]
    cols = lax.axis_size(COL)
    share = width // cols
    *pieces, own_features = gather(grad_out, features)
    smem, vmem = pl.BlockSpec(memory_space=pltpu.SMEM), pl.BlockSpec(memory_space=pltpu.VMEM)
    anywhere = pl.BlockSpec(memory_space=pl.ANY)
    parts, shares = pl.pallas_call(
        tiles_kernel,
        out_shape=(
            jax.ShapeDtypeStruct((cols, tile, width), jnp.bfloat16),
            jax.ShapeDtypeStruct((cols, share, width), jnp.bfloat16),
        ),
        in_specs=[smem] * 3 + [vmem] + [anywhere] * len(pieces) + [vmem],
        out_specs=(vmem, vmem),
        scratch_shapes=[
            pltpu.VMEM((lax.axis_size(ROW), tile, width), jnp.bfloat16),
            pltpu.VMEM((cols, tile, width), jnp.float32),
            pltpu.SemaphoreType.DMA((len(pieces),)),
        ],
        compiler_params=pltpu.CompilerParams(vmem_limit_bytes=24 * 2**20),
    )(
        tile_count[0],
        tile_rows[0, 0],
        place_of(tile_cols[0, 0]),
        tile_values[0, 0],
        *pieces,
        own_features,
    )
    shares = lax.all_to_all(shares, COL, 0, 0, tiled=True)

    def summed(kernel, shape, dtype, array, scale=1.0):
        return pl.pallas_call(
            functools.partial(kernel, scale),
            out_shape=jax.ShapeDtypeStruct(shape, dtype),
            in_specs=[vmem],
            out_specs=vmem,
            compiler_params=pltpu.CompilerParams(vmem_limit_bytes=4 * 2**20),
        )(array)

    near, far = "zb", ("za", "core")
    shares = summed(sum_and_copy_kernel, (lax.axis_size(near), share, width), jnp.float32, shares, nodes**-0.5)
    grad_share = summed(sum_kernel, (share, width), jnp.float32, lax.all_to_all(shares, near, 0, 0, tiled=True))
    grad_share, parts = lax.optimization_barrier((grad_share, parts))
    parts = lax.all_to_all(parts, COL, 0, 0, tiled=True)
    shares, parts = lax.optimization_barrier((lax.all_gather(grad_share, far), parts))
    shares = summed(sum_and_copy_kernel, (cols, share, width), jnp.bfloat16, shares)
    weight_grad = lax.all_to_all(shares, COL, 0, 0, tiled=True).reshape(width, width).astype(jnp.float32)
    input_grad = pl.pallas_call(
        finish_kernel,
        out_shape=jax.ShapeDtypeStruct((tile, width), jnp.bfloat16),
        in_specs=[vmem] * 2,
        out_specs=vmem,
        compiler_params=pltpu.CompilerParams(vmem_limit_bytes=8 * 2**20),
    )(parts, weight)
    return input_grad, weight_grad


def solution(mesh):
    fine = Mesh(mesh.devices.reshape(8, 4, 2, 4, 4), ROW + COL)
    placed = (
        P(COL + ROW, None),
        P(ROW + COL, None),
        P(),
        P(ROW, COL, None, None, None),
        P(ROW, COL, None),
        P(ROW, COL, None),
        P(ROW, COL),
    )

    def whole(grad_out, *rest):
        return jax.shard_map(
            functools.partial(body, grad_out.shape[0]),
            mesh=fine,
            in_specs=placed,
            out_specs=(P(ROW + COL, None), P()),
            check_vma=False,
        )(grad_out, *rest)

    return whole
```
